32 devices in a mesh: space: 8 (over z, y), dp: 4 (over x, core).
Axes of the slice: x: 2, y: 2, z: 4, core: 2. Of those that a mesh axis runs over, the one named last changes fastest.
Arguments:
- features: bfloat16 [4, 4096, 128], P('dp', 'space'), may hold values from -6 to 6
- occupancy: int32 [4, 4096], P('dp', 'space'), may hold values from 0 to 1
- brick_pairs: int32 [4, 64, 27], P('dp', 'space'), may hold values from 0 to 24, as said below
- send_lists: int32 [4, 8, 16], P('dp', 'space'), may hold values from -1 to 7, as said below
- scan_weight: int32 [4], P('dp'), may hold values from 1 to 12
- kernel: bfloat16 [3456, 128], replicated, may hold values from -0.109375 to 0.109375
- cotangent: bfloat16 [4, 4096, 128], P('dp', 'space'), may hold values from -6 to 6
Outputs:
- output_features: bfloat16 [4, 4096, 128], P('dp', 'space')
- grad_features: bfloat16 [4, 4096, 128], P('dp', 'space')
- grad_kernel: float32 [3456, 128], replicated
The draws below stay inside these ranges and needn't reach their ends.
Inputs may be any that keep to these rules, and one draw needn't show every extreme that they name: `brick_pairs`: entry 13 of brick b is b itself. A value under 8 is a brick of the same owner; 8 + t * 2 + k names entry k of what owner t sends to this owner, and then t differs from this owner's index on space in exactly one bit; 24 is an empty brick. `send_lists`: for a destination t that differs from the owner's index in exactly one bit, 2 distinct slots of the owner; for every other destination all -1.
All inputs are finite; a program needn't handle non-finite values.
Results may differ from the reference program's by a relative error of at most 0.0017.
Values may be sent and summed in bfloat16 or wider, within the bound.
A program may use at most 64 MiB of HBM per device.

```python
import math
import jax
import jax.numpy as jnp
import numpy as np
from jax import lax

C = 128
BRICK_DEV = 8
PEER_CAP = 2
LEVELS = 3
BRICKS = 64
N_SPACE = 8
N_DP = 4


def brick_tables(key):
    key_list = jax.random.split(key, 8)
    slot_ids = jnp.arange(BRICK_DEV, dtype=jnp.int32)
    space_ids = jnp.arange(N_SPACE, dtype=jnp.int32)
    live_count = jax.random.randint(key_list[0], (N_DP, N_SPACE), BRICK_DEV // 2, BRICK_DEV + 1)
    live_brick = slot_ids[None, None, :] < live_count[:, :, None]
    thresh = jax.random.randint(key_list[1], (N_DP, N_SPACE, BRICK_DEV, 1), 3, 10)
    coin_toss = jax.random.randint(key_list[2], (N_DP, N_SPACE, BRICK_DEV, 64), 0, 10)
    occupied = jnp.logical_and(coin_toss < thresh, live_brick[:, :, :, None]).astype(jnp.int32)
    sort_score = jax.random.randint(key_list[3], (N_DP, N_SPACE, N_SPACE, BRICK_DEV), 0, 1 << 20) * (2 * BRICK_DEV) + slot_ids + jnp.where(live_brick[:, :, None, :], 0, 1 << 30)
    permuted = jnp.argsort(sort_score, axis=-1)[..., :PEER_CAP].astype(jnp.int32)
    index_gap = jnp.bitwise_xor(space_ids[:, None], space_ids[None, :])
    one_bit = jnp.logical_and(index_gap > 0, jnp.bitwise_and(index_gap, index_gap - 1) == 0)
    send_table = jnp.where(one_bit[None, :, :, None], permuted, -1).reshape(N_DP, N_SPACE, N_SPACE * PEER_CAP).astype(jnp.int32)
    pair_shape = (N_DP, N_SPACE, BRICK_DEV, 27)
    category = jax.random.randint(key_list[4], pair_shape, 0, 10)
    local_pick = jax.random.randint(key_list[5], pair_shape, 0, BRICK_DEV) % live_count[:, :, None, None]
    bit_pick = jax.random.randint(key_list[6], pair_shape, 0, LEVELS)
    slot_pick = jax.random.randint(key_list[7], pair_shape, 0, PEER_CAP)
    partner = jnp.bitwise_xor(space_ids[None, :, None, None], jnp.left_shift(jnp.ones_like(bit_pick), bit_pick))
    zero_index = BRICK_DEV + N_SPACE * PEER_CAP
    neighbour = jnp.where(category < 3, zero_index, jnp.where(category < 6, local_pick, BRICK_DEV + partner * PEER_CAP + slot_pick))
    neighbour = jnp.where(live_brick[:, :, :, None], neighbour, zero_index)
    centre = jnp.broadcast_to(slot_ids[None, None, :, None], pair_shape)
    column_ids = jnp.arange(27, dtype=jnp.int32)
    neighbour = jnp.where(column_ids == 13, centre, neighbour).astype(jnp.int32)
    return (occupied.reshape(N_DP, N_SPACE * BRICK_DEV * 64), neighbour.reshape(N_DP, N_SPACE * BRICK_DEV, 27), send_table)


def draw_occupancy(key, part):
    return brick_tables(jax.random.fold_in(key, 17))[0]


def draw_brick_pairs(key, part):
    return brick_tables(jax.random.fold_in(key, 17))[1]


def draw_send_lists(key, part):
    return brick_tables(jax.random.fold_in(key, 17))[2]


def draw_scan_weight(key, part):
    scan_ids = jnp.arange(N_DP, dtype=jnp.int32)
    raised = jax.random.randint(jax.random.fold_in(key, 29), (N_DP,), 1, 4) + 3 * scan_ids
    return jnp.where(scan_ids == N_DP - 1, 3 * N_DP, raised).astype(jnp.int32)


def block_levels(stream_key, shape, cuts, low, high):
    def one(position, parts):
        draws = jax.random.uniform(jax.random.fold_in(jax.random.fold_in(stream_key, 6), position), (parts,), jnp.float32, low / len(cuts), high / len(cuts))
        return jnp.repeat(jnp.exp(draws), shape[position] // parts).reshape((-1,) + (1,) * (len(shape) - position - 1))

    gain = one(*cuts[0])
    for cut in cuts[1:]:
        gain = gain * one(*cut)
    return gain


def bell_draw(rng, extent, spread, bound, shards=(), kind=jnp.bfloat16):
    factor_of = block_levels(rng, extent, shards, -0.22, 0.18) if shards else 1.0
    entries = jax.random.normal(rng, extent, jnp.float32) * spread * factor_of
    return jnp.minimum(jnp.maximum(entries, -bound), bound).astype(kind)


def setup_inputs(seed: int = 0) -> dict:
    key_of = jax.random.split(jax.random.key(seed), 8)
    return {
        "features": bell_draw(key_of[0], (N_DP, BRICKS * 64, C), 1.0, 6.0, ((0, 4), (1, 8))),
        "occupancy": draw_occupancy(jax.random.fold_in(key_of[7], 71), 0),
        "brick_pairs": draw_brick_pairs(jax.random.fold_in(key_of[7], 71), 0),
        "send_lists": draw_send_lists(jax.random.fold_in(key_of[7], 71), 0),
        "scan_weight": draw_scan_weight(jax.random.fold_in(key_of[7], 71), 0),
        "kernel": bell_draw(key_of[5], (27 * C, C), (27 * C) ** -0.5, 0.109375),
        "cotangent": bell_draw(key_of[6], (N_DP, BRICKS * 64, C), 1.0, 6.0, ((0, 4), (1, 8))),
    }


def patch_layout():
    offset_list = []
    inner_list = []
    for pos_x in range(6):
        for pos_y in range(6):
            for pos_z in range(6):
                offset_parts = []
                inner_parts = []
                for coordinate in (pos_x, pos_y, pos_z):
                    shifted = coordinate - 1
                    brick_step = shifted // 4
                    offset_parts.append(brick_step + 1)
                    inner_parts.append(shifted - 4 * brick_step)
                offset_list.append(9 * offset_parts[0] + 3 * offset_parts[1] + offset_parts[2])
                inner_list.append(16 * inner_parts[0] + 4 * inner_parts[1] + inner_parts[2])
    return (np.array(offset_list, np.int32), np.array(inner_list, np.int32))

def convolve(table_rows, table_index, grad_in, kernel, offset_map, inner_map):
    bricks = table_index.shape[0]
    channels = table_rows.shape[1]
    patch_rows = (table_index[:, offset_map] * 64 + inner_map[None, :]).astype(jnp.int32)
    patch_cube = jnp.take(table_rows, patch_rows.reshape(-1), axis=0).reshape(bricks, 6, 6, 6, channels)
    result = jnp.zeros((bricks * 64, channels), jnp.float32)
    patch_grad = jnp.zeros((bricks, 6, 6, 6, channels), jnp.float32)
    weight_grads = []
    for shift_x in range(3):
        pieces = []
        for tap_index in range(9):
            shift_y = tap_index // 3
            shift_z = tap_index % 3
            pieces.append(patch_cube[:, shift_x:shift_x + 4, shift_y:shift_y + 4, shift_z:shift_z + 4, :].reshape(bricks * 64, channels))
        columns = jnp.concatenate(pieces, axis=1)
        kernel_rows = kernel[shift_x * 9 * channels:(shift_x + 1) * 9 * channels]
        result = result + jnp.dot(columns, kernel_rows, preferred_element_type=jnp.float32)
        weight_grads.append(jnp.dot(columns.T, grad_in, preferred_element_type=jnp.float32))
        for tap_index in range(9):
            shift_y = tap_index // 3
            shift_z = tap_index % 3
            tap_weight = kernel_rows[tap_index * channels:(tap_index + 1) * channels]
            tap_grad = jnp.dot(grad_in, tap_weight.T, preferred_element_type=jnp.float32)
            patch_grad = patch_grad.at[:, shift_x:shift_x + 4, shift_y:shift_y + 4, shift_z:shift_z + 4, :].add(tap_grad.reshape(bricks, 4, 4, 4, channels))
    table_grad = jax.ops.segment_sum(patch_grad.reshape(-1, channels), patch_rows.reshape(-1), num_segments=table_rows.shape[0])
    return (result, table_grad, jnp.concatenate(weight_grads, axis=0))

def halo_index(pair_table, device, bricks, nspace, peer_cap, levels):
    zero_full = bricks + nspace * peer_cap
    relative = jnp.clip(pair_table - bricks, 0, nspace * peer_cap - 1)
    source = relative // peer_cap
    within = relative % peer_cap
    flipped = jnp.bitwise_xor(source, device)
    level_of = jnp.zeros_like(pair_table)
    for bit_level in range(levels):
        level_of = level_of + bit_level * (flipped == 1 << bit_level).astype(jnp.int32)
    compact = bricks + level_of * peer_cap + within
    outside = bricks + levels * peer_cap
    return jnp.where(pair_table < bricks, pair_table, jnp.where(pair_table >= zero_full, outside, compact)).astype(jnp.int32)

def reference(features, occupancy, brick_pairs, send_lists, scan_weight, kernel, cotangent):
    offset_list, inner_list = patch_layout()
    offset_map = jnp.asarray(offset_list, jnp.int32)
    inner_map = jnp.asarray(inner_list, jnp.int32)
    weight_total = jnp.sum(scan_weight.astype(jnp.float32))
    devices = jnp.arange(N_SPACE, dtype=jnp.int32)
    slot_ids = jnp.arange(PEER_CAP, dtype=jnp.int32)
    own_rows = BRICK_DEV * 64
    outputs = []
    feature_grads = []
    kernel_grad = jnp.zeros((27 * C, C), jnp.float32)
    for scan_index in range(N_DP):
        voxel_mask = occupancy[scan_index].reshape(N_SPACE, own_rows, 1).astype(jnp.bfloat16)
        masked = features[scan_index].reshape(N_SPACE, own_rows, C) * voxel_mask
        grad_in = cotangent[scan_index].reshape(N_SPACE, own_rows, C) * voxel_mask
        brick_rows = masked.reshape(N_SPACE, BRICK_DEV, 64 * C)
        send_table = send_lists[scan_index]
        pieces = []
        for bit_level in range(LEVELS):
            partner = jnp.bitwise_xor(devices, 1 << bit_level)
            chosen = send_table[partner[:, None], devices[:, None] * PEER_CAP + slot_ids[None, :]]
            gathered = brick_rows[partner[:, None], jnp.maximum(chosen, 0)]
            pieces.append(jnp.where((chosen >= 0)[:, :, None], gathered, jnp.zeros_like(gathered)))
        empty_brick = jnp.zeros((N_SPACE, 1, 64 * C), jnp.bfloat16)
        brick_table = jnp.concatenate([brick_rows] + pieces + [empty_brick], axis=1).reshape(N_SPACE, -1, C)
        table_index = halo_index(brick_pairs[scan_index].reshape(N_SPACE, BRICK_DEV, 27), devices[:, None, None], BRICK_DEV, N_SPACE, PEER_CAP, LEVELS)

        def per_device(carried, inputs):
            table_rows, device_index, device_grad = inputs
            result, table_grad, weight_grad = convolve(table_rows, device_index, device_grad, kernel, offset_map, inner_map)
            return (carried + weight_grad, (result, table_grad))
        scan_grad, (conv_out, table_grads) = lax.scan(per_device, jnp.zeros((27 * C, C), jnp.float32), (brick_table, table_index, grad_in))
        own_grad = table_grads[:, :own_rows]
        halo_grads = table_grads[:, own_rows:own_rows + LEVELS * PEER_CAP * 64].astype(jnp.bfloat16).reshape(N_SPACE, LEVELS * PEER_CAP, 64 * C)
        collected = jnp.zeros((N_SPACE * BRICK_DEV + 1, 64 * C), jnp.float32)
        for bit_level in range(LEVELS):
            partner = jnp.bitwise_xor(devices, 1 << bit_level)
            grad_piece = halo_grads[partner, bit_level * PEER_CAP:(bit_level + 1) * PEER_CAP]
            chosen = send_table[devices[:, None], partner[:, None] * PEER_CAP + slot_ids[None, :]]
            target = jnp.where(chosen >= 0, devices[:, None] * BRICK_DEV + chosen, N_SPACE * BRICK_DEV).astype(jnp.int32)
            collected = collected + jax.ops.segment_sum(grad_piece.astype(jnp.float32).reshape(-1, 64 * C), target.reshape(-1), num_segments=N_SPACE * BRICK_DEV + 1)
        returned = collected[:-1].reshape(N_SPACE, own_rows, C)
        grad_sum = grad_in.astype(jnp.float32) + own_grad + returned
        factor = scan_weight[scan_index].astype(jnp.float32) * N_DP / weight_total
        mask_float = voxel_mask.astype(jnp.float32)
        outputs.append((mask_float * (conv_out + masked.astype(jnp.float32))).astype(jnp.bfloat16).reshape(N_SPACE * own_rows, C))
        feature_grads.append((factor * (mask_float * grad_sum)).astype(jnp.bfloat16).reshape(N_SPACE * own_rows, C))
        kernel_grad = kernel_grad + factor * scan_grad
    kernel_grad = kernel_grad / math.sqrt(64.0 * BRICKS)
    return (jnp.stack(outputs), jnp.stack(feature_grads), kernel_grad)
```

```python
import functools
import math

import jax
import jax.numpy as jnp
import numpy as np
from jax import lax
from jax.experimental import pallas as pl
from jax.experimental.pallas import tpu as pltpu
from jax.sharding import PartitionSpec as P

MESH = pl.DeviceIdType.MESH
VOXELS = 64
TAPS = 27


def axis_places(step):
    return {-1: [(0, 3)], 0: [(1, 0), (2, 1), (3, 2), (4, 3)], 1: [(5, 0)]}[step]


def slab(offset):
    steps = (offset // 9 - 1, offset // 3 % 3 - 1, offset % 3 - 1)
    places = []
    for px, vx in axis_places(steps[0]):
        for py, vy in axis_places(steps[1]):
            for pz, vz in axis_places(steps[2]):
                places.append(((px, py, pz), 16 * vx + 4 * vy + vz))
    return places


def voxel_classes():
    readers = {}
    for offset in range(TAPS):
        for pos, voxel in slab(offset):
            readers.setdefault(voxel, []).append((offset, pos))
    classes = {}
    for voxel in range(VOXELS):
        key = tuple(o for o, _ in readers[voxel])
        classes.setdefault(key, []).append((voxel, [pos for _, pos in readers[voxel]]))
    return classes


def kernel_body(sizes, scale, feat, occ, pairs_s, pairs_v, sends, weight, ker, cot,
                out_f, out_g, out_k,
                mask, fnat, table, gnat, gvox, patch, pgrad, cols, tgrad, conv, wgrad,
                halo_out, halo_in, back_out, back_in, wsend, wrecv,
                core_in, half_in, tail_in, tail_sum, send_sem, recv_sem):
    nspace, ndp, cap, bricks, chan = sizes
    ls, ld = nspace.bit_length() - 1, ndp.bit_length() - 1
    own = bricks * VOXELS
    index = {"space": lax.axis_index("space"), "dp": lax.axis_index("dp")}

    def bit_of(bit):
        axis, level = bit
        return lax.rem(index[axis] // (1 << level), 2)

    def peer_index(bit):
        return index[bit[0]] + (1 - 2 * bit_of(bit)) * (1 << bit[1])

    all_bits = [("dp", i) for i in range(ld)] + [("space", i) for i in range(ls)]
    barrier = pltpu.get_barrier_semaphore()
    for bit in all_bits:
        pl.semaphore_signal(barrier, inc=1, device_id={bit[0]: peer_index(bit)},
                            device_id_type=MESH)

    started = []

    def send(src, dst, bit):
        n = len(started)
        copy = pltpu.make_async_remote_copy(
            src_ref=src, dst_ref=dst, send_sem=send_sem.at[n], recv_sem=recv_sem.at[n],
            device_id={bit[0]: peer_index(bit)}, device_id_type=MESH)
        copy.start()
        started.append(copy)
        return copy

    for i in range(own // 128):
        row = occ[0:1, i * 128:(i + 1) * 128].astype(jnp.float32)
        mask[i * 128:(i + 1) * 128, :] = jnp.transpose(jnp.broadcast_to(row, (128, 128)))
    fnat[...] = feat[0].astype(jnp.float32) * mask[...]
    table[0:bricks] = fnat[...].reshape(bricks, VOXELS, chan)
    table[bricks + nspace * cap] = jnp.zeros((VOXELS, chan), jnp.float32)

    picks = []
    for level in range(ls):
        partner = peer_index(("space", level))
        for k in range(cap):
            chosen = sends[0, 0, partner * cap + k]
            picks.append(chosen)
            live = jnp.full((VOXELS, chan), chosen, jnp.int32) >= 0
            at = (level * cap + k) * VOXELS
            brick = table[jnp.maximum(chosen, 0)]
            halo_out[at:at + VOXELS, :] = jnp.where(live, brick, 0.0).astype(jnp.bfloat16)
    own_weight = weight[0].astype(jnp.float32)
    wsend[0] = jnp.full((8, 128), own_weight, jnp.float32)

    pl.semaphore_wait(barrier, len(all_bits))
    rows = cap * VOXELS
    halo = [send(halo_out.at[pl.ds(level * rows, rows)], halo_in.at[pl.ds(level * rows, rows)],
                 ("space", level)) for level in range(ls)]
    wcopy = send(wsend.at[0], wrecv.at[0], ("dp", 0))

    gnat[...] = cot[0].astype(jnp.float32) * mask[...]
    for v in range(VOXELS):
        gvox[v * 8:(v + 1) * 8, :] = gnat[pl.ds(v, bricks, stride=VOXELS), :]
    grad = gvox[...].astype(jnp.bfloat16)
    for pos, v in slab(13):
        patch[pos[0], pos[1], pos[2]] = fnat[pl.ds(v, bricks, stride=VOXELS), :]
    pgrad[...] = jnp.zeros(pgrad.shape, jnp.float32)

    def spread(taps):
        for tap in taps:
            a, b, c = tap // 9, tap // 3 % 3, tap % 3
            part = lax.dot_general(grad, ker[tap * chan:(tap + 1) * chan, :],
                                   (((1,), (1,)), ((), ())), preferred_element_type=jnp.float32)
            pgrad[a:a + 4, b:b + 4, c:c + 4] += part.reshape(4, 4, 4, bricks, chan)

    spread(range(0, 9))

    for level in range(ls):
        halo[level].wait_recv()
        entry = bricks + peer_index(("space", level)) * cap
        for k in range(cap):
            at = level * rows + k * VOXELS
            table[entry + k] = halo_in[at:at + VOXELS, :].astype(jnp.float32)
    for level in range(ld):
        wcopy.wait_recv()
        wsend[level + 1] = wsend[level] + wrecv[level]
        if level + 1 < ld:
            wcopy = send(wsend.at[level + 1], wrecv.at[level + 1], ("dp", level + 1))
    for b in range(bricks):
        for offset in range(TAPS):
            if offset != 13:
                entry = pairs_s[0, b, offset]
                for pos, v in slab(offset):
                    patch[pos[0], pos[1], pos[2], b:b + 1, :] = table[entry, v:v + 1, :]

    for tap in range(TAPS):
        a, b, c = tap // 9, tap // 3 % 3, tap % 3
        cols[:, tap * chan:(tap + 1) * chan] = patch[a:a + 4, b:b + 4, c:c + 4].reshape(
            own, chan).astype(jnp.bfloat16)

    total_rows = TAPS * chan
    half_rows = total_rows // 2
    part_rows = half_rows // 3
    first, rest = all_bits[0], all_bits[1:]
    turn, tail = rest[:3], rest[3:]
    orders = [[turn[(p + j) % 3] for j in range(3)] for p in range(3)]
    mine = bit_of(first)

    def weigh(taps):
        lo, hi = taps[0] * chan, (taps[-1] + 1) * chan
        wgrad[lo:hi, :] = own_weight * lax.dot_general(
            cols[:, lo:hi], grad, (((0,), (0,)), ((), ())), preferred_element_type=jnp.float32)

    def tile8(x):
        return pl.multiple_of(x, 8)

    cores = []
    done = 0
    for p in range(3):
        low_end = -(-(p + 1) * part_rows // chan)
        mid = half_rows // chan
        high_end = -(-(half_rows + (p + 1) * part_rows) // chan)
        low_end = min(low_end, mid)
        if p == 0:
            low_at, high_at = 0, mid
        if low_end > low_at:
            weigh(list(range(low_at, low_end)))
        weigh(list(range(high_at, high_end)))
        low_at, high_at = low_end, high_end
        src = tile8((1 - mine) * half_rows + p * part_rows)
        cores.append(send(wgrad.at[pl.ds(src, part_rows)], core_in.at[p], first))

    offs = [mine * half_rows + p * part_rows for p in range(3)]
    flight = list(cores)
    width = part_rows

    def reduce_stage(j):
        for p in range(3):
            flight[p].wait_recv()
            size = part_rows >> min(j, 3)
            off = tile8(offs[p])
            if j == 0:
                wgrad[pl.ds(off, size), :] += core_in[p]
            elif j <= 3:
                at = part_rows - (part_rows >> (j - 1))
                wgrad[pl.ds(off, size), :] += half_in[p, at:at + size, :]
            else:
                i = j - 4
                held = wgrad[pl.ds(off, size), :] if i == 0 else tail_sum[p, i - 1]
                tail_sum[p, i] = held + tail_in[p, i]
            if j < 3:
                bit = orders[p][j]
                half = size // 2
                at = part_rows - (part_rows >> j)
                other = tile8(offs[p] + (1 - bit_of(bit)) * half)
                flight[p] = send(wgrad.at[pl.ds(other, half)],
                                 half_in.at[p, pl.ds(at, half)], bit)
                offs[p] = offs[p] + bit_of(bit) * half
            elif j - 3 < len(tail):
                i = j - 3
                src = wgrad.at[pl.ds(off, size)] if i == 0 else tail_sum.at[p, i - 1]
                flight[p] = send(src, tail_in.at[p, i], tail[i])

    reduce_stage(0)
    spread(range(9, 18))
    reduce_stage(1)
    spread(range(18, 27))

    entries = tgrad.shape[0] // VOXELS
    lane = lax.broadcasted_iota(jnp.int32, (1, 128), 1)
    code = jnp.where(lane < bricks, lane, -1)
    for level in range(ls):
        for k in range(cap):
            name = bricks + peer_index(("space", level)) * cap + k
            code = jnp.where(lane == bricks + level * cap + k, name, code)
    hits = {}
    for offset in range(TAPS):
        hit = pairs_v[0, :, offset:offset + 1] == code
        hits[offset] = jnp.where(hit, 1.0, 0.0).astype(jnp.float32)
    for offsets, voxels in voxel_classes().items():
        left = jnp.concatenate([hits[o] for o in offsets] * 2, axis=0).astype(jnp.bfloat16)
        right = jnp.concatenate(
            [jnp.concatenate([pgrad[pos[j][0], pos[j][1], pos[j][2]] for _, pos in voxels], axis=1)
             for j in range(len(offsets))], axis=0)
        high = right.astype(jnp.bfloat16)
        low = (right - high.astype(jnp.float32)).astype(jnp.bfloat16)
        sums = lax.dot_general(left, jnp.concatenate([high, low], axis=0),
                               (((0,), (0,)), ((), ())), preferred_element_type=jnp.float32)
        for n, (v, _) in enumerate(voxels):
            for t in range(0, entries, 8):
                tgrad[pl.ds(t * VOXELS + v, 8, stride=VOXELS), :] = sums[t:t + 8,
                                                                        n * chan:(n + 1) * chan]
    back_out[...] = tgrad[own:own + ls * rows, :].astype(jnp.bfloat16)
    back = [send(back_out.at[pl.ds(level * rows, rows)], back_in.at[pl.ds(level * rows, rows)],
                 ("space", level)) for level in range(ls)]

    reduce_stage(2)
    third = TAPS // 3 * chan

    def convolve(i):
        return jnp.dot(cols[:, i * third:(i + 1) * third], ker[i * third:(i + 1) * third, :],
                       preferred_element_type=jnp.float32)

    conv[...] = convolve(0) + patch[1:5, 1:5, 1:5].reshape(own, chan)
    reduce_stage(3)
    conv[...] += convolve(1)
    for j in range(len(tail)):
        reduce_stage(4 + j)
    total = wsend[ld][0:1, :]
    last = part_rows >> 3
    kernel_scale = (ndp / total) * scale
    for p in range(3):
        off = tile8(offs[p])
        held = tail_sum[p, len(tail) - 1] if tail else wgrad[pl.ds(off, last), :]
        out_k[pl.ds(off, last), :] = held * kernel_scale

    def gather_start(j):
        for p in range(3):
            size = part_rows >> j
            off = tile8(offs[p])
            bit = orders[p][j - 1] if j else first
            flight[p] = send(out_k.at[pl.ds(off, size)], out_k.at[pl.ds(off, size)], bit)
            if j:
                offs[p] = offs[p] - bit_of(bit) * size

    def gather_wait():
        for p in range(3):
            flight[p].wait_recv()

    gather_start(3)
    conv[...] += convolve(2)
    gather_wait()
    gather_start(2)
    for v in range(VOXELS):
        gvox[pl.ds(v, bricks, stride=VOXELS), :] = conv[v * 8:(v + 1) * 8, :]
    out_f[0] = (gvox[...] * mask[...]).astype(jnp.bfloat16)
    gather_wait()
    gather_start(1)
    for copy in back:
        copy.wait_recv()
    factor = own_weight * ndp / total
    for b in range(bricks):
        lo, hi = b * VOXELS, (b + 1) * VOXELS
        held = gnat[lo:hi, :] + tgrad[lo:hi, :]
        for e, chosen in enumerate(picks):
            came = back_in[e * VOXELS:(e + 1) * VOXELS, :].astype(jnp.float32)
            here = jnp.full((VOXELS, chan), chosen, jnp.int32) == b
            held = held + jnp.where(here, came, 0.0)
        out_g[0, lo:hi, :] = (factor * (mask[lo:hi, :] * held)).astype(jnp.bfloat16)
    gather_wait()
    gather_start(0)
    gather_wait()
    for copy in started:
        copy.wait_send()


def on_device(features, occupancy, brick_pairs, send_lists, scan_weight, kernel, cotangent):
    nspace, ndp = lax.axis_size("space"), lax.axis_size("dp")
    own, chan = features.shape[1:]
    bricks = own // VOXELS
    cap = send_lists.shape[2] // nspace
    ls, ld = nspace.bit_length() - 1, ndp.bit_length() - 1
    entries = -(-(bricks + ls * cap) // 8) * 8
    rows = TAPS * chan
    part = rows // 6
    tail = max(ls + ld - 4, 1)
    copies = 2 * ls + ld + 3 * (1 + 3 + (ls + ld - 4) + 4)
    f32, bf16 = jnp.float32, jnp.bfloat16
    vmem, smem = pl.BlockSpec(memory_space=pltpu.VMEM), pl.BlockSpec(memory_space=pltpu.SMEM)
    scale = 1.0 / math.sqrt(64.0 * bricks * nspace)
    return pl.pallas_call(
        functools.partial(kernel_body, (nspace, ndp, cap, bricks, chan), scale),
        out_shape=(
            jax.ShapeDtypeStruct(features.shape, bf16),
            jax.ShapeDtypeStruct(features.shape, bf16),
            jax.ShapeDtypeStruct((rows, chan), f32),
        ),
        in_specs=[vmem, vmem, smem, vmem, smem, smem, vmem, vmem],
        out_specs=(vmem, vmem, vmem),
        scratch_shapes=[
            pltpu.VMEM((own, chan), f32),
            pltpu.VMEM((own, chan), f32),
            pltpu.VMEM((bricks + nspace * cap + 1, VOXELS, chan), f32),
            pltpu.VMEM((own, chan), f32),
            pltpu.VMEM((own, chan), f32),
            pltpu.VMEM((6, 6, 6, bricks, chan), f32),
            pltpu.VMEM((6, 6, 6, bricks, chan), f32),
            pltpu.VMEM((own, rows), bf16),
            pltpu.VMEM((entries * VOXELS, chan), f32),
            pltpu.VMEM((own, chan), f32),
            pltpu.VMEM((rows, chan), f32),
            pltpu.VMEM((ls * cap * VOXELS, chan), bf16),
            pltpu.VMEM((ls * cap * VOXELS, chan), bf16),
            pltpu.VMEM((ls * cap * VOXELS, chan), bf16),
            pltpu.VMEM((ls * cap * VOXELS, chan), bf16),
            pltpu.VMEM((ld + 1, 8, 128), f32),
            pltpu.VMEM((ld, 8, 128), f32),
            pltpu.VMEM((3, part, chan), f32),
            pltpu.VMEM((3, part, chan), f32),
            pltpu.VMEM((3, tail, part // 8, chan), f32),
            pltpu.VMEM((3, tail, part // 8, chan), f32),
            pltpu.SemaphoreType.DMA((copies,)),
            pltpu.SemaphoreType.DMA((copies,)),
        ],
        compiler_params=pltpu.CompilerParams(
            collective_id=0, has_side_effects=True, vmem_limit_bytes=50 * 1024 * 1024
        ),
        cost_estimate=pl.CostEstimate(flops=6 * own * rows * chan, bytes_accessed=6 * 2**20,
                                      transcendentals=0),
    )(features, occupancy, brick_pairs, brick_pairs, send_lists, scan_weight, kernel, cotangent)


def solution(mesh):
    return jax.shard_map(
        on_device,
        mesh=mesh,
        in_specs=(
            P("dp", "space", None),
            P("dp", "space"),
            P("dp", "space", None),
            P("dp", "space", None),
            P("dp"),
            P(),
            P("dp", "space", None),
        ),
        out_specs=(P("dp", "space", None), P("dp", "space", None), P()),
        check_vma=False,
    )
```

```python
import functools
import math

import jax
import jax.numpy as jnp
import numpy as np
from jax import lax
from jax.experimental import pallas as pl
from jax.experimental.pallas import tpu as pltpu
from jax.sharding import PartitionSpec as P

MESH = pl.DeviceIdType.MESH
VOXELS = 64
TAPS = 27
VMEM_GRANT = 64 * 2**20 - 2**16


def axis_places(step):
    return {-1: [(0, 3)], 0: [(1, 0), (2, 1), (3, 2), (4, 3)], 1: [(5, 0)]}[step]


def slab(offset):
    steps = (offset // 9 - 1, offset // 3 % 3 - 1, offset % 3 - 1)
    places = []
    for px, vx in axis_places(steps[0]):
        for py, vy in axis_places(steps[1]):
            for pz, vz in axis_places(steps[2]):
                places.append(((px, py, pz), 16 * vx + 4 * vy + vz))
    return places


def voxel_classes():
    readers = {}
    for offset in range(TAPS):
        for pos, voxel in slab(offset):
            readers.setdefault(voxel, []).append((offset, pos))
    classes = {}
    for voxel in range(VOXELS):
        key = tuple(o for o, _ in readers[voxel])
        classes.setdefault(key, []).append((voxel, [pos for _, pos in readers[voxel]]))
    return classes


def kernel_body(sizes, scale, feat_h, occ_h, pairs_h, sends_h, weight_h, ker_h, cot_h,
                home_f, home_g, home_k, out_f, out_g, out_k,
                feat, occ, pairs_s, pairs_v, sends, weight, ker, cot, load_sem,
                mask, fnat, table, gnat, gvox, patch, pgrad, cols, tgrad, conv, wgrad,
                halo_out, halo_in, back_out, back_in, wsend, wrecv,
                core_in, half_in, tail_in, tail_sum, send_sem, recv_sem):
    nspace, ndp, cap, bricks, chan = sizes
    ls, ld = nspace.bit_length() - 1, ndp.bit_length() - 1
    own = bricks * VOXELS
    index = {"space": lax.axis_index("space"), "dp": lax.axis_index("dp")}

    def bit_of(bit):
        axis, level = bit
        return lax.rem(index[axis] // (1 << level), 2)

    def peer_index(bit):
        return index[bit[0]] + (1 - 2 * bit_of(bit)) * (1 << bit[1])

    loads = {}
    for n, (name, src, dst) in enumerate([
            ("occ", occ_h, occ), ("feat", feat_h, feat), ("sends", sends_h, sends),
            ("weight", weight_h, weight), ("cot", cot_h, cot), ("pairs_s", pairs_h, pairs_s),
            ("pairs_v", pairs_h, pairs_v), ("ker", ker_h, ker)]):
        loads[name] = pltpu.make_async_copy(src, dst, load_sem.at[n])
        loads[name].start()

    all_bits = [("dp", i) for i in range(ld)] + [("space", i) for i in range(ls)]
    barrier = pltpu.get_barrier_semaphore()
    for bit in all_bits:
        pl.semaphore_signal(barrier, inc=1, device_id={bit[0]: peer_index(bit)},
                            device_id_type=MESH)

    started = []

    def send(src, dst, bit):
        n = len(started)
        copy = pltpu.make_async_remote_copy(
            src_ref=src, dst_ref=dst, send_sem=send_sem.at[n], recv_sem=recv_sem.at[n],
            device_id={bit[0]: peer_index(bit)}, device_id_type=MESH)
        copy.start()
        started.append(copy)
        return copy

    loads["occ"].wait()
    for i in range(own // 128):
        row = occ[0:1, i * 128:(i + 1) * 128].astype(jnp.float32)
        mask[i * 128:(i + 1) * 128, :] = jnp.transpose(jnp.broadcast_to(row, (128, 128)))
    loads["feat"].wait()
    fnat[...] = feat[0].astype(jnp.float32) * mask[...]
    table[0:bricks] = fnat[...].reshape(bricks, VOXELS, chan)
    table[bricks + nspace * cap] = jnp.zeros((VOXELS, chan), jnp.float32)

    loads["sends"].wait()
    loads["weight"].wait()
    picks = []
    for level in range(ls):
        partner = peer_index(("space", level))
        for k in range(cap):
            chosen = sends[0, 0, partner * cap + k]
            picks.append(chosen)
            live = jnp.full((VOXELS, chan), chosen, jnp.int32) >= 0
            at = (level * cap + k) * VOXELS
            brick = table[jnp.maximum(chosen, 0)]
            halo_out[at:at + VOXELS, :] = jnp.where(live, brick, 0.0).astype(jnp.bfloat16)
    own_weight = weight[0].astype(jnp.float32)
    wsend[0] = jnp.full((8, 128), own_weight, jnp.float32)

    pl.semaphore_wait(barrier, len(all_bits))
    rows = cap * VOXELS
    halo = [send(halo_out.at[pl.ds(level * rows, rows)], halo_in.at[pl.ds(level * rows, rows)],
                 ("space", level)) for level in range(ls)]
    wcopy = send(wsend.at[0], wrecv.at[0], ("dp", 0))

    loads["cot"].wait()
    gnat[...] = cot[0].astype(jnp.float32) * mask[...]
    for v in range(VOXELS):
        gvox[v * 8:(v + 1) * 8, :] = gnat[pl.ds(v, bricks, stride=VOXELS), :]
    grad = gvox[...].astype(jnp.bfloat16)
    grad_t = jnp.transpose(gvox[...]).astype(jnp.bfloat16)
    for pos, v in slab(13):
        patch[pos[0], pos[1], pos[2]] = fnat[pl.ds(v, bricks, stride=VOXELS), :]
    pgrad[...] = jnp.zeros(pgrad.shape, jnp.float32)

    def spread(taps):
        for tap in taps:
            a, b, c = tap // 9, tap // 3 % 3, tap % 3
            part = lax.dot_general(grad, ker[tap * chan:(tap + 1) * chan, :],
                                   (((1,), (1,)), ((), ())), preferred_element_type=jnp.float32)
            pgrad[a:a + 4, b:b + 4, c:c + 4] += part.reshape(4, 4, 4, bricks, chan)

    loads["ker"].wait()
    spread(range(0, 9))

    for level in range(ls):
        halo[level].wait_recv()
        entry = bricks + peer_index(("space", level)) * cap
        for k in range(cap):
            at = level * rows + k * VOXELS
            table[entry + k] = halo_in[at:at + VOXELS, :].astype(jnp.float32)
    for level in range(ld):
        wcopy.wait_recv()
        wsend[level + 1] = wsend[level] + wrecv[level]
        if level + 1 < ld:
            wcopy = send(wsend.at[level + 1], wrecv.at[level + 1], ("dp", level + 1))
    loads["pairs_s"].wait()
    for b in range(bricks):
        for offset in range(TAPS):
            if offset != 13:
                entry = pairs_s[0, b, offset]
                for pos, v in slab(offset):
                    patch[pos[0], pos[1], pos[2], b:b + 1, :] = table[entry, v:v + 1, :]

    for tap in range(TAPS):
        a, b, c = tap // 9, tap // 3 % 3, tap % 3
        cols[:, tap * chan:(tap + 1) * chan] = patch[a:a + 4, b:b + 4, c:c + 4].reshape(
            own, chan).astype(jnp.bfloat16)

    total_rows = TAPS * chan
    half_rows = total_rows // 2
    part_rows = half_rows // 3
    first, rest = all_bits[0], all_bits[1:]
    turn, tail = rest[:3], rest[3:]
    orders = [[turn[(p + j) % 3] for j in range(3)] for p in range(3)]
    mine = bit_of(first)

    def weigh(taps):
        lo, hi = taps[0] * chan, (taps[-1] + 1) * chan
        turned = own_weight * jnp.dot(grad_t, cols[:, lo:hi], preferred_element_type=jnp.float32)
        for n, tap in enumerate(taps):
            wgrad[tap * chan:(tap + 1) * chan, :] = turned[:, n * chan:(n + 1) * chan]

    def tile8(x):
        return pl.multiple_of(x, 8)

    units = part_rows // 64
    sizes_of = [(units + 1) // 2 * 64, units // 2 * 64]
    starts_of = [0, sizes_of[0]]
    offs = {(p, s): mine * half_rows + p * part_rows + starts_of[s]
            for s in range(2) for p in range(3)}
    flight = {}
    low_at, high_at = 0, half_rows // chan
    for p in range(3):
        low_end = min(-(-(p + 1) * part_rows // chan), half_rows // chan)
        high_end = -(-(half_rows + (p + 1) * part_rows) // chan)
        weigh(list(range(low_at, low_end)))
        weigh(list(range(high_at, high_end)))
        low_at, high_at = low_end, high_end
        for s in range(2):
            src = tile8((1 - mine) * half_rows + p * part_rows + starts_of[s])
            flight[p, s] = send(wgrad.at[pl.ds(src, sizes_of[s])],
                                core_in.at[p, pl.ds(starts_of[s], sizes_of[s])], first)

    def reduce_stage(j, s):
        for p in range(3):
            flight[p, s].wait_recv()
            size = sizes_of[s] >> min(j, 3)
            off = tile8(offs[p, s])
            tail_at = starts_of[s] >> 3
            if j == 0:
                wgrad[pl.ds(off, size), :] += core_in[p, starts_of[s]:starts_of[s] + size, :]
            elif j <= 3:
                at = starts_of[s] + sizes_of[s] - (sizes_of[s] >> (j - 1))
                wgrad[pl.ds(off, size), :] += half_in[p, at:at + size, :]
            else:
                i = j - 4
                held = (wgrad[pl.ds(off, size), :] if i == 0
                        else tail_sum[p, i - 1, tail_at:tail_at + size, :])
                tail_sum[p, i, tail_at:tail_at + size, :] = (
                    held + tail_in[p, i, tail_at:tail_at + size, :])
            if j < 3:
                bit = orders[p][j]
                half = size // 2
                at = starts_of[s] + sizes_of[s] - (sizes_of[s] >> j)
                other = tile8(offs[p, s] + (1 - bit_of(bit)) * half)
                flight[p, s] = send(wgrad.at[pl.ds(other, half)],
                                    half_in.at[p, pl.ds(at, half)], bit)
                offs[p, s] = offs[p, s] + bit_of(bit) * half
            elif j - 3 < len(tail):
                i = j - 3
                src = (wgrad.at[pl.ds(off, size)] if i == 0
                       else tail_sum.at[p, i - 1, pl.ds(tail_at, size)])
                flight[p, s] = send(src, tail_in.at[p, i, pl.ds(tail_at, size)], tail[i])

    spread(range(9, 18))
    reduce_stage(0, 0)
    reduce_stage(0, 1)
    spread(range(18, 27))
    reduce_stage(1, 0)
    reduce_stage(1, 1)

    entries = tgrad.shape[0] // VOXELS
    lane = lax.broadcasted_iota(jnp.int32, (1, 128), 1)
    code = jnp.where(lane < bricks, lane, -1)
    for level in range(ls):
        for k in range(cap):
            name = bricks + peer_index(("space", level)) * cap + k
            code = jnp.where(lane == bricks + level * cap + k, name, code)
    loads["pairs_v"].wait()
    hits = {}
    for offset in range(TAPS):
        hit = pairs_v[0, :, offset:offset + 1] == code
        hits[offset] = jnp.where(hit, 1.0, 0.0).astype(jnp.float32)
    for turn_of, (offsets, voxels) in enumerate(voxel_classes().items()):
        if turn_of == 14:
            reduce_stage(2, 0)
        left = jnp.concatenate([hits[o] for o in offsets] * 2, axis=0).astype(jnp.bfloat16)
        right = jnp.concatenate(
            [jnp.concatenate([pgrad[pos[j][0], pos[j][1], pos[j][2]] for _, pos in voxels], axis=1)
             for j in range(len(offsets))], axis=0)
        high = right.astype(jnp.bfloat16)
        low = (right - high.astype(jnp.float32)).astype(jnp.bfloat16)
        sums = lax.dot_general(left, jnp.concatenate([high, low], axis=0),
                               (((0,), (0,)), ((), ())), preferred_element_type=jnp.float32)
        for n, (v, _) in enumerate(voxels):
            for t in range(0, entries, 8):
                tgrad[pl.ds(t * VOXELS + v, 8, stride=VOXELS), :] = sums[t:t + 8,
                                                                        n * chan:(n + 1) * chan]
    back_out[...] = tgrad[own:own + ls * rows, :].astype(jnp.bfloat16)
    back = [send(back_out.at[pl.ds(level * rows, rows)], back_in.at[pl.ds(level * rows, rows)],
                 ("space", level)) for level in range(ls)]

    reduce_stage(2, 1)
    third = TAPS // 3 * chan

    def convolve(i):
        return jnp.dot(cols[:, i * third:(i + 1) * third], ker[i * third:(i + 1) * third, :],
                       preferred_element_type=jnp.float32)

    total = wsend[ld][0:1, :]
    kernel_scale = (ndp / total) * scale

    def gather_start(j, s):
        for p in range(3):
            size = sizes_of[s] >> j
            off = tile8(offs[p, s])
            bit = orders[p][j - 1] if j else first
            flight[p, s] = send(out_k.at[pl.ds(off, size)], out_k.at[pl.ds(off, size)], bit)
            if j:
                offs[p, s] = offs[p, s] - bit_of(bit) * size

    def gather_wait(s):
        for p in range(3):
            flight[p, s].wait_recv()

    def finish(s):
        for j in range(len(tail)):
            reduce_stage(4 + j, s)
        last = sizes_of[s] >> 3
        tail_at = starts_of[s] >> 3
        for p in range(3):
            off = tile8(offs[p, s])
            held = (tail_sum[p, len(tail) - 1, tail_at:tail_at + last, :] if tail
                    else wgrad[pl.ds(off, last), :])
            out_k[pl.ds(off, last), :] = held * kernel_scale
        gather_start(3, s)

    conv[...] = convolve(0) + patch[1:5, 1:5, 1:5].reshape(own, chan)
    reduce_stage(3, 0)
    conv[...] += convolve(1)
    reduce_stage(3, 1)
    conv[...] += convolve(2)
    for v in range(VOXELS):
        gvox[pl.ds(v, bricks, stride=VOXELS), :] = conv[v * 8:(v + 1) * 8, :]
    out_f[0] = (gvox[...] * mask[...]).astype(jnp.bfloat16)
    homes = [pltpu.make_async_copy(out_f, home_f, load_sem.at[8])]
    homes[0].start()
    finish(0)
    for copy in back:
        copy.wait_recv()
    factor = own_weight * ndp / total

    def feature_grads(some):
        for b in some:
            lo, hi = b * VOXELS, (b + 1) * VOXELS
            held = gnat[lo:hi, :] + tgrad[lo:hi, :]
            for e, chosen in enumerate(picks):
                came = back_in[e * VOXELS:(e + 1) * VOXELS, :].astype(jnp.float32)
                here = jnp.full((VOXELS, chan), chosen, jnp.int32) == b
                held = held + jnp.where(here, came, 0.0)
            out_g[0, lo:hi, :] = (factor * (mask[lo:hi, :] * held)).astype(jnp.bfloat16)

    feature_grads(range(bricks // 2))
    finish(1)
    feature_grads(range(bricks // 2, bricks))
    homes.append(pltpu.make_async_copy(out_g, home_g, load_sem.at[9]))
    homes[1].start()
    for j in (2, 1, 0):
        for s in range(2):
            gather_wait(s)
            gather_start(j, s)
    for n, half in enumerate((mine, 1 - mine)):
        if n == 1:
            gather_wait(0)
            gather_wait(1)
        at = pl.ds(tile8(half * half_rows), half_rows)
        homes.append(pltpu.make_async_copy(out_k.at[at], home_k.at[at], load_sem.at[10 + n]))
        homes[-1].start()
    for copy in homes:
        copy.wait()
    for copy in started:
        copy.wait_send()


def write_out(in_f, in_g, in_k, out_f, out_g, out_k, held, turned, sems):
    chan = in_k.shape[1]
    copies = [pltpu.make_async_copy(in_f, out_f, sems.at[0]),
              pltpu.make_async_copy(in_g, out_g, sems.at[1])]
    loads = []
    for n in range(3):
        at = pl.ds(n * TAPS // 3 * chan, TAPS // 3 * chan)
        loads.append(pltpu.make_async_copy(in_k.at[at], held.at[at], sems.at[2 + n]))
    for copy in loads + copies:
        copy.start()
    for n in range(3):
        lo, hi = n * TAPS // 3, (n + 1) * TAPS // 3
        loads[n].wait()
        for tap in range(lo, hi):
            at = slice(tap * chan, (tap + 1) * chan)
            turned[at, :] = jnp.transpose(held[at, :])
        at = pl.ds(lo * chan, (hi - lo) * chan)
        copies.append(pltpu.make_async_copy(turned.at[at], out_k.at[at], sems.at[5 + n]))
        copies[-1].start()
    for copy in copies:
        copy.wait()


def on_device(features, occupancy, brick_pairs, send_lists, scan_weight, kernel, cotangent):
    nspace, ndp = lax.axis_size("space"), lax.axis_size("dp")
    own, chan = features.shape[1:]
    bricks = own // VOXELS
    cap = send_lists.shape[2] // nspace
    ls, ld = nspace.bit_length() - 1, ndp.bit_length() - 1
    entries = -(-(bricks + ls * cap) // 8) * 8
    rows = TAPS * chan
    part = rows // 6
    tail = max(ls + ld - 4, 1)
    copies = 2 * ls + ld + 6 * (1 + 3 + (ls + ld - 4) + 4)
    f32, bf16 = jnp.float32, jnp.bfloat16
    i32 = jnp.int32
    hbm = pl.BlockSpec(memory_space=pltpu.HBM)
    scale = 1.0 / math.sqrt(64.0 * bricks * nspace)
    results = pl.pallas_call(
        functools.partial(kernel_body, (nspace, ndp, cap, bricks, chan), scale),
        out_shape=(
            jax.ShapeDtypeStruct(features.shape, bf16),
            jax.ShapeDtypeStruct(features.shape, bf16),
            jax.ShapeDtypeStruct((rows, chan), f32),
        ),
        in_specs=[hbm] * 7,
        out_specs=(hbm, hbm, hbm),
        scratch_shapes=[
            pltpu.VMEM(features.shape, bf16),
            pltpu.VMEM(features.shape, bf16),
            pltpu.VMEM((rows, chan), f32),
            pltpu.VMEM(features.shape, bf16),
            pltpu.VMEM(occupancy.shape, i32),
            pltpu.SMEM(brick_pairs.shape, i32),
            pltpu.VMEM(brick_pairs.shape, i32),
            pltpu.SMEM(send_lists.shape, i32),
            pltpu.SMEM(scan_weight.shape, i32),
            pltpu.VMEM(kernel.shape, bf16),
            pltpu.VMEM(cotangent.shape, bf16),
            pltpu.SemaphoreType.DMA((12,)),
            pltpu.VMEM((own, chan), f32),
            pltpu.VMEM((own, chan), f32),
            pltpu.VMEM((bricks + nspace * cap + 1, VOXELS, chan), f32),
            pltpu.VMEM((own, chan), f32),
            pltpu.VMEM((own, chan), f32),
            pltpu.VMEM((6, 6, 6, bricks, chan), f32),
            pltpu.VMEM((6, 6, 6, bricks, chan), f32),
            pltpu.VMEM((own, rows), bf16),
            pltpu.VMEM((entries * VOXELS, chan), f32),
            pltpu.VMEM((own, chan), f32),
            pltpu.VMEM((rows, chan), f32),
            pltpu.VMEM((ls * cap * VOXELS, chan), bf16),
            pltpu.VMEM((ls * cap * VOXELS, chan), bf16),
            pltpu.VMEM((ls * cap * VOXELS, chan), bf16),
            pltpu.VMEM((ls * cap * VOXELS, chan), bf16),
            pltpu.VMEM((ld + 1, 8, 128), f32),
            pltpu.VMEM((ld, 8, 128), f32),
            pltpu.VMEM((3, part, chan), f32),
            pltpu.VMEM((3, part, chan), f32),
            pltpu.VMEM((3, tail, part // 8, chan), f32),
            pltpu.VMEM((3, tail, part // 8, chan), f32),
            pltpu.SemaphoreType.DMA((copies,)),
            pltpu.SemaphoreType.DMA((copies,)),
        ],
        compiler_params=pltpu.CompilerParams(
            collective_id=0, has_side_effects=True, vmem_limit_bytes=VMEM_GRANT
        ),
        cost_estimate=pl.CostEstimate(flops=6 * own * rows * chan, bytes_accessed=6 * 2**20,
                                      transcendentals=0),
    )(features, occupancy, brick_pairs, send_lists, scan_weight, kernel, cotangent)
    return pl.pallas_call(
        write_out,
        out_shape=tuple(jax.ShapeDtypeStruct(r.shape, r.dtype) for r in results),
        in_specs=[hbm] * 3,
        out_specs=(hbm, hbm, hbm),
        scratch_shapes=[pltpu.VMEM((rows, chan), f32), pltpu.VMEM((rows, chan), f32),
                        pltpu.SemaphoreType.DMA((8,))],
        compiler_params=pltpu.CompilerParams(vmem_limit_bytes=VMEM_GRANT),
        cost_estimate=pl.CostEstimate(flops=0, bytes_accessed=4 * 2**20, transcendentals=0),
    )(*results)


def solution(mesh):
    return jax.shard_map(
        on_device,
        mesh=mesh,
        in_specs=(
            P("dp", "space", None),
            P("dp", "space"),
            P("dp", "space", None),
            P("dp", "space", None),
            P("dp"),
            P(),
            P("dp", "space", None),
        ),
        out_specs=(P("dp", "space", None), P("dp", "space", None), P()),
        check_vma=False,
    )
```

```python
import functools
import math

import jax
import jax.numpy as jnp
import numpy as np
from jax import lax
from jax.experimental import pallas as pl
from jax.experimental.pallas import tpu as pltpu
from jax.sharding import PartitionSpec as P

MESH = pl.DeviceIdType.MESH
VOXELS = 64
TAPS = 27
VMEM_GRANT = 64 * 2**20 - 2**16


def axis_places(step):
    return {-1: [(0, 3)], 0: [(1, 0), (2, 1), (3, 2), (4, 3)], 1: [(5, 0)]}[step]


def slab(offset):
    steps = (offset // 9 - 1, offset // 3 % 3 - 1, offset % 3 - 1)
    places = []
    for px, vx in axis_places(steps[0]):
        for py, vy in axis_places(steps[1]):
            for pz, vz in axis_places(steps[2]):
                places.append(((px, py, pz), 16 * vx + 4 * vy + vz))
    return places


def voxel_classes():
    readers = {}
    for offset in range(TAPS):
        for pos, voxel in slab(offset):
            readers.setdefault(voxel, []).append((offset, pos))
    classes = {}
    for voxel in range(VOXELS):
        key = tuple(o for o, _ in readers[voxel])
        classes.setdefault(key, []).append((voxel, [pos for _, pos in readers[voxel]]))
    return classes


def kernel_body(sizes, scale, feat_h, occ_h, pairs_h, sends_h, weight_h, ker_h, cot_h,
                home_f, home_g, home_k, out_f, out_g, out_k,
                feat, occ, pairs_s, pairs_v, sends, weight, ker, cot, load_sem,
                mask, fnat, table, gnat, gvox, patch, pgrad, cols, tgrad, conv, wgrad,
                halo_out, halo_in, back_out, back_in, wsend, wrecv,
                core_in, half_in, tail_in, tail_sum, send_sem, recv_sem):
    nspace, ndp, cap, bricks, chan = sizes
    ls, ld = nspace.bit_length() - 1, ndp.bit_length() - 1
    own = bricks * VOXELS
    index = {"space": lax.axis_index("space"), "dp": lax.axis_index("dp")}

    def bit_of(bit):
        axis, level = bit
        return lax.rem(index[axis] // (1 << level), 2)

    def peer_index(bit):
        return index[bit[0]] + (1 - 2 * bit_of(bit)) * (1 << bit[1])

    loads = {}
    for n, (name, src, dst) in enumerate([
            ("occ", occ_h, occ), ("feat", feat_h, feat), ("sends", sends_h, sends),
            ("weight", weight_h, weight), ("cot", cot_h, cot), ("pairs_s", pairs_h, pairs_s),
            ("pairs_v", pairs_h, pairs_v), ("ker", ker_h, ker)]):
        loads[name] = pltpu.make_async_copy(src, dst, load_sem.at[n])
        loads[name].start()

    all_bits = [("dp", i) for i in range(ld)] + [("space", i) for i in range(ls)]
    barrier = pltpu.get_barrier_semaphore()
    for bit in all_bits:
        pl.semaphore_signal(barrier, inc=1, device_id={bit[0]: peer_index(bit)},
                            device_id_type=MESH)

    started = []

    def send(src, dst, bit):
        n = len(started)
        copy = pltpu.make_async_remote_copy(
            src_ref=src, dst_ref=dst, send_sem=send_sem.at[n], recv_sem=recv_sem.at[n],
            device_id={bit[0]: peer_index(bit)}, device_id_type=MESH)
        copy.start()
        started.append(copy)
        return copy

    loads["occ"].wait()
    for i in range(own // 128):
        row = occ[0:1, i * 128:(i + 1) * 128].astype(jnp.float32)
        mask[i * 128:(i + 1) * 128, :] = jnp.transpose(jnp.broadcast_to(row, (128, 128)))
    loads["feat"].wait()
    fnat[...] = feat[0].astype(jnp.float32) * mask[...]
    table[0:bricks] = fnat[...].reshape(bricks, VOXELS, chan)
    table[bricks + nspace * cap] = jnp.zeros((VOXELS, chan), jnp.float32)

    loads["sends"].wait()
    loads["weight"].wait()
    picks = []
    for level in range(ls):
        partner = peer_index(("space", level))
        for k in range(cap):
            chosen = sends[0, 0, partner * cap + k]
            picks.append(chosen)
            live = jnp.full((VOXELS, chan), chosen, jnp.int32) >= 0
            at = (level * cap + k) * VOXELS
            brick = table[jnp.maximum(chosen, 0)]
            halo_out[at:at + VOXELS, :] = jnp.where(live, brick, 0.0).astype(jnp.bfloat16)
    own_weight = weight[0].astype(jnp.float32)
    wsend[0] = jnp.full((8, 128), own_weight, jnp.float32)

    pl.semaphore_wait(barrier, len(all_bits))
    rows = cap * VOXELS
    halo = [send(halo_out.at[pl.ds(level * rows, rows)], halo_in.at[pl.ds(level * rows, rows)],
                 ("space", level)) for level in range(ls)]
    wcopy = send(wsend.at[0], wrecv.at[0], ("dp", 0))

    loads["cot"].wait()
    gnat[...] = cot[0].astype(jnp.float32) * mask[...]
    for v in range(VOXELS):
        gvox[v * 8:(v + 1) * 8, :] = gnat[pl.ds(v, bricks, stride=VOXELS), :]
    grad = gvox[...].astype(jnp.bfloat16)
    for pos, v in slab(13):
        patch[pos[0], pos[1], pos[2]] = fnat[pl.ds(v, bricks, stride=VOXELS), :]
    pgrad[...] = jnp.zeros(pgrad.shape, jnp.float32)

    def spread(taps):
        for tap in taps:
            a, b, c = tap // 9, tap // 3 % 3, tap % 3
            part = lax.dot_general(grad, ker[tap * chan:(tap + 1) * chan, :],
                                   (((1,), (1,)), ((), ())), preferred_element_type=jnp.float32)
            pgrad[a:a + 4, b:b + 4, c:c + 4] += part.reshape(4, 4, 4, bricks, chan)

    loads["ker"].wait()
    spread(range(0, 9))

    for level in range(ls):
        halo[level].wait_recv()
        entry = bricks + peer_index(("space", level)) * cap
        for k in range(cap):
            at = level * rows + k * VOXELS
            table[entry + k] = halo_in[at:at + VOXELS, :].astype(jnp.float32)
    for level in range(ld):
        wcopy.wait_recv()
        wsend[level + 1] = wsend[level] + wrecv[level]
        if level + 1 < ld:
            wcopy = send(wsend.at[level + 1], wrecv.at[level + 1], ("dp", level + 1))
    loads["pairs_s"].wait()
    for b in range(bricks):
        for offset in range(TAPS):
            if offset != 13:
                entry = pairs_s[0, b, offset]
                for pos, v in slab(offset):
                    patch[pos[0], pos[1], pos[2], b:b + 1, :] = table[entry, v:v + 1, :]

    for tap in range(TAPS):
        a, b, c = tap // 9, tap // 3 % 3, tap % 3
        cols[:, tap * chan:(tap + 1) * chan] = patch[a:a + 4, b:b + 4, c:c + 4].reshape(
            own, chan).astype(jnp.bfloat16)

    total_rows = TAPS * chan
    half_rows = total_rows // 2
    part_rows = half_rows // 3
    first, rest = all_bits[0], all_bits[1:]
    turn, tail = rest[:3], rest[3:]
    orders = [[turn[(p + j) % 3] for j in range(3)] for p in range(3)]
    mine = bit_of(first)

    def weigh(taps):
        lo, hi = taps[0] * chan, (taps[-1] + 1) * chan
        wgrad[lo:hi, :] = own_weight * lax.dot_general(
            cols[:, lo:hi], grad, (((0,), (0,)), ((), ())), preferred_element_type=jnp.float32)

    def tile8(x):
        return pl.multiple_of(x, 8)

    units = part_rows // 64
    sizes_of = [(units + 1) // 2 * 64, units // 2 * 64]
    starts_of = [0, sizes_of[0]]
    offs = {(p, s): mine * half_rows + p * part_rows + starts_of[s]
            for s in range(2) for p in range(3)}
    flight = {}
    def reduce_stage(j, s, parts=range(3)):
        for p in parts:
            flight[p, s].wait_recv()
            size = sizes_of[s] >> min(j, 3)
            off = tile8(offs[p, s])
            tail_at = starts_of[s] >> 3
            if j == 0:
                wgrad[pl.ds(off, size), :] += core_in[p, starts_of[s]:starts_of[s] + size, :]
            elif j <= 3:
                at = starts_of[s] + sizes_of[s] - (sizes_of[s] >> (j - 1))
                wgrad[pl.ds(off, size), :] += half_in[p, at:at + size, :]
            else:
                i = j - 4
                held = (wgrad[pl.ds(off, size), :] if i == 0
                        else tail_sum[p, i - 1, tail_at:tail_at + size, :])
                tail_sum[p, i, tail_at:tail_at + size, :] = (
                    held + tail_in[p, i, tail_at:tail_at + size, :])
            if j < 3:
                bit = orders[p][j]
                half = size // 2
                at = starts_of[s] + sizes_of[s] - (sizes_of[s] >> j)
                other = tile8(offs[p, s] + (1 - bit_of(bit)) * half)
                flight[p, s] = send(wgrad.at[pl.ds(other, half)],
                                    half_in.at[p, pl.ds(at, half)], bit)
                offs[p, s] = offs[p, s] + bit_of(bit) * half
            elif j - 3 < len(tail):
                i = j - 3
                src = (wgrad.at[pl.ds(off, size)] if i == 0
                       else tail_sum.at[p, i - 1, pl.ds(tail_at, size)])
                flight[p, s] = send(src, tail_in.at[p, i, pl.ds(tail_at, size)], tail[i])

    for p in range(3):
        if p > 1:
            reduce_stage(0, 0, [p - 2])
            reduce_stage(0, 1, [p - 2])
        low_at = min(-(-p * part_rows // chan), half_rows // chan)
        high_at = -(-(half_rows + p * part_rows) // chan) if p else half_rows // chan
        low_end = min(-(-(p + 1) * part_rows // chan), half_rows // chan)
        high_end = -(-(half_rows + (p + 1) * part_rows) // chan)
        weigh(list(range(low_at, low_end)))
        weigh(list(range(high_at, high_end)))
        for s in range(2):
            src = tile8((1 - mine) * half_rows + p * part_rows + starts_of[s])
            flight[p, s] = send(wgrad.at[pl.ds(src, sizes_of[s])],
                                core_in.at[p, pl.ds(starts_of[s], sizes_of[s])], first)

    reduce_stage(0, 0, [1])
    reduce_stage(0, 1, [1])
    spread(range(9, 13))
    reduce_stage(0, 0, [2])
    reduce_stage(0, 1, [2])
    spread(range(13, 18))
    reduce_stage(1, 0)
    spread(range(18, 23))
    reduce_stage(1, 1)
    spread(range(23, 27))

    entries = tgrad.shape[0] // VOXELS
    lane = lax.broadcasted_iota(jnp.int32, (1, 128), 1)
    code = jnp.where(lane < bricks, lane, -1)
    for level in range(ls):
        for k in range(cap):
            name = bricks + peer_index(("space", level)) * cap + k
            code = jnp.where(lane == bricks + level * cap + k, name, code)
    loads["pairs_v"].wait()
    hits = {}
    for offset in range(TAPS):
        hit = pairs_v[0, :, offset:offset + 1] == code
        hits[offset] = jnp.where(hit, 1.0, 0.0).astype(jnp.float32)
    for turn_of, (offsets, voxels) in enumerate(voxel_classes().items()):
        if turn_of == 14:
            reduce_stage(2, 0)
        left = jnp.concatenate([hits[o] for o in offsets] * 2, axis=0).astype(jnp.bfloat16)
        right = jnp.concatenate(
            [jnp.concatenate([pgrad[pos[j][0], pos[j][1], pos[j][2]] for _, pos in voxels], axis=1)
             for j in range(len(offsets))], axis=0)
        high = right.astype(jnp.bfloat16)
        low = (right - high.astype(jnp.float32)).astype(jnp.bfloat16)
        sums = lax.dot_general(left, jnp.concatenate([high, low], axis=0),
                               (((0,), (0,)), ((), ())), preferred_element_type=jnp.float32)
        for n, (v, _) in enumerate(voxels):
            for t in range(0, entries, 8):
                tgrad[pl.ds(t * VOXELS + v, 8, stride=VOXELS), :] = sums[t:t + 8,
                                                                        n * chan:(n + 1) * chan]
    back_out[...] = tgrad[own:own + ls * rows, :].astype(jnp.bfloat16)
    back = [send(back_out.at[pl.ds(level * rows, rows)], back_in.at[pl.ds(level * rows, rows)],
                 ("space", level)) for level in range(ls)]

    reduce_stage(2, 1)
    third = TAPS // 3 * chan

    def convolve(i):
        return jnp.dot(cols[:, i * third:(i + 1) * third], ker[i * third:(i + 1) * third, :],
                       preferred_element_type=jnp.float32)

    total = wsend[ld][0:1, :]
    kernel_scale = (ndp / total) * scale

    def gather_start(j, s):
        for p in range(3):
            size = sizes_of[s] >> j
            off = tile8(offs[p, s])
            bit = orders[p][j - 1] if j else first
            flight[p, s] = send(out_k.at[pl.ds(off, size)], out_k.at[pl.ds(off, size)], bit)
            if j:
                offs[p, s] = offs[p, s] - bit_of(bit) * size

    def gather_wait(s):
        for p in range(3):
            flight[p, s].wait_recv()

    def finish(s):
        for j in range(len(tail)):
            reduce_stage(4 + j, s)
        last = sizes_of[s] >> 3
        tail_at = starts_of[s] >> 3
        for p in range(3):
            off = tile8(offs[p, s])
            held = (tail_sum[p, len(tail) - 1, tail_at:tail_at + last, :] if tail
                    else wgrad[pl.ds(off, last), :])
            out_k[pl.ds(off, last), :] = held * kernel_scale
        gather_start(3, s)

    conv[...] = convolve(0) + patch[1:5, 1:5, 1:5].reshape(own, chan)
    reduce_stage(3, 0)
    conv[...] += convolve(1)
    reduce_stage(3, 1)
    conv[...] += convolve(2)
    for v in range(VOXELS):
        gvox[pl.ds(v, bricks, stride=VOXELS), :] = conv[v * 8:(v + 1) * 8, :]
    out_f[0] = (gvox[...] * mask[...]).astype(jnp.bfloat16)
    homes = [pltpu.make_async_copy(out_f, home_f, load_sem.at[8])]
    homes[0].start()
    finish(0)
    for copy in back:
        copy.wait_recv()
    factor = own_weight * ndp / total

    def feature_grads(some):
        for b in some:
            lo, hi = b * VOXELS, (b + 1) * VOXELS
            held = gnat[lo:hi, :] + tgrad[lo:hi, :]
            for e, chosen in enumerate(picks):
                came = back_in[e * VOXELS:(e + 1) * VOXELS, :].astype(jnp.float32)
                here = jnp.full((VOXELS, chan), chosen, jnp.int32) == b
                held = held + jnp.where(here, came, 0.0)
            out_g[0, lo:hi, :] = (factor * (mask[lo:hi, :] * held)).astype(jnp.bfloat16)

    feature_grads(range(bricks // 2))
    finish(1)
    feature_grads(range(bricks // 2, bricks))
    homes.append(pltpu.make_async_copy(out_g, home_g, load_sem.at[9]))
    homes[1].start()
    for j in (2, 1, 0):
        for s in range(2):
            gather_wait(s)
            gather_start(j, s)
    for n, half in enumerate((mine, 1 - mine)):
        if n == 1:
            gather_wait(0)
            gather_wait(1)
        at = pl.ds(tile8(half * half_rows), half_rows)
        homes.append(pltpu.make_async_copy(out_k.at[at], home_k.at[at], load_sem.at[10 + n]))
        homes[-1].start()
    for copy in homes:
        copy.wait()
    for copy in started:
        copy.wait_send()


def write_out(in_f, in_g, in_k, out_f, out_g, out_k, held_f, held_g, held_k, sems):
    rows = in_k.shape[0] // 4
    moves = [(in_f, held_f, out_f), (in_g, held_g, out_g)]
    for n in range(4):
        at = pl.ds(n * rows, rows)
        moves.append((in_k.at[at], held_k.at[at], out_k.at[at]))
    loads = [pltpu.make_async_copy(src, held, sems.at[2 * n])
             for n, (src, held, _) in enumerate(moves)]
    for copy in loads:
        copy.start()
    stores = [pltpu.make_async_copy(held, dst, sems.at[2 * n + 1])
              for n, (_, held, dst) in enumerate(moves)]
    for load, store in zip(loads, stores):
        load.wait()
        store.start()
    for copy in stores:
        copy.wait()


def on_device(features, occupancy, brick_pairs, send_lists, scan_weight, kernel, cotangent):
    nspace, ndp = lax.axis_size("space"), lax.axis_size("dp")
    own, chan = features.shape[1:]
    bricks = own // VOXELS
    cap = send_lists.shape[2] // nspace
    ls, ld = nspace.bit_length() - 1, ndp.bit_length() - 1
    entries = -(-(bricks + ls * cap) // 8) * 8
    rows = TAPS * chan
    part = rows // 6
    tail = max(ls + ld - 4, 1)
    copies = 2 * ls + ld + 6 * (1 + 3 + (ls + ld - 4) + 4)
    f32, bf16 = jnp.float32, jnp.bfloat16
    i32 = jnp.int32
    hbm = pl.BlockSpec(memory_space=pltpu.HBM)
    scale = 1.0 / math.sqrt(64.0 * bricks * nspace)
    results = pl.pallas_call(
        functools.partial(kernel_body, (nspace, ndp, cap, bricks, chan), scale),
        out_shape=(
            jax.ShapeDtypeStruct(features.shape, bf16),
            jax.ShapeDtypeStruct(features.shape, bf16),
            jax.ShapeDtypeStruct((rows, chan), f32),
        ),
        in_specs=[hbm] * 7,
        out_specs=(hbm, hbm, hbm),
        scratch_shapes=[
            pltpu.VMEM(features.shape, bf16),
            pltpu.VMEM(features.shape, bf16),
            pltpu.VMEM((rows, chan), f32),
            pltpu.VMEM(features.shape, bf16),
            pltpu.VMEM(occupancy.shape, i32),
            pltpu.SMEM(brick_pairs.shape, i32),
            pltpu.VMEM(brick_pairs.shape, i32),
            pltpu.SMEM(send_lists.shape, i32),
            pltpu.SMEM(scan_weight.shape, i32),
            pltpu.VMEM(kernel.shape, bf16),
            pltpu.VMEM(cotangent.shape, bf16),
            pltpu.SemaphoreType.DMA((12,)),
            pltpu.VMEM((own, chan), f32),
            pltpu.VMEM((own, chan), f32),
            pltpu.VMEM((bricks + nspace * cap + 1, VOXELS, chan), f32),
            pltpu.VMEM((own, chan), f32),
            pltpu.VMEM((own, chan), f32),
            pltpu.VMEM((6, 6, 6, bricks, chan), f32),
            pltpu.VMEM((6, 6, 6, bricks, chan), f32),
            pltpu.VMEM((own, rows), bf16),
            pltpu.VMEM((entries * VOXELS, chan), f32),
            pltpu.VMEM((own, chan), f32),
            pltpu.VMEM((rows, chan), f32),
            pltpu.VMEM((ls * cap * VOXELS, chan), bf16),
            pltpu.VMEM((ls * cap * VOXELS, chan), bf16),
            pltpu.VMEM((ls * cap * VOXELS, chan), bf16),
            pltpu.VMEM((ls * cap * VOXELS, chan), bf16),
            pltpu.VMEM((ld + 1, 8, 128), f32),
            pltpu.VMEM((ld, 8, 128), f32),
            pltpu.VMEM((3, part, chan), f32),
            pltpu.VMEM((3, part, chan), f32),
            pltpu.VMEM((3, tail, part // 8, chan), f32),
            pltpu.VMEM((3, tail, part // 8, chan), f32),
            pltpu.SemaphoreType.DMA((copies,)),
            pltpu.SemaphoreType.DMA((copies,)),
        ],
        compiler_params=pltpu.CompilerParams(
            collective_id=0, has_side_effects=True, vmem_limit_bytes=VMEM_GRANT
        ),
        cost_estimate=pl.CostEstimate(flops=6 * own * rows * chan, bytes_accessed=6 * 2**20,
                                      transcendentals=0),
    )(features, occupancy, brick_pairs, send_lists, scan_weight, kernel, cotangent)
    return pl.pallas_call(
        write_out,
        out_shape=tuple(jax.ShapeDtypeStruct(r.shape, r.dtype) for r in results),
        in_specs=[hbm] * 3,
        out_specs=(hbm, hbm, hbm),
        scratch_shapes=[pltpu.VMEM(features.shape, bf16), pltpu.VMEM(features.shape, bf16),
                        pltpu.VMEM((rows, chan), f32), pltpu.SemaphoreType.DMA((12,))],
        compiler_params=pltpu.CompilerParams(vmem_limit_bytes=VMEM_GRANT),
        cost_estimate=pl.CostEstimate(flops=0, bytes_accessed=4 * 2**20, transcendentals=0),
    )(*results)


def solution(mesh):
    return jax.shard_map(
        on_device,
        mesh=mesh,
        in_specs=(
            P("dp", "space", None),
            P("dp", "space"),
            P("dp", "space", None),
            P("dp", "space", None),
            P("dp"),
            P(),
            P("dp", "space", None),
        ),
        out_specs=(P("dp", "space", None), P("dp", "space", None), P()),
        check_vma=False,
    )
```

```python
import functools
import math

import jax
import jax.numpy as jnp
import numpy as np
from jax import lax
from jax.experimental import pallas as pl
from jax.experimental.pallas import tpu as pltpu
from jax.sharding import PartitionSpec as P

MESH = pl.DeviceIdType.MESH
VOXELS = 64
TAPS = 27
VMEM_GRANT = 64 * 2**20 - 2**16


def axis_places(step):
    return {-1: [(0, 3)], 0: [(1, 0), (2, 1), (3, 2), (4, 3)], 1: [(5, 0)]}[step]


def slab(offset):
    steps = (offset // 9 - 1, offset // 3 % 3 - 1, offset % 3 - 1)
    places = []
    for px, vx in axis_places(steps[0]):
        for py, vy in axis_places(steps[1]):
            for pz, vz in axis_places(steps[2]):
                places.append(((px, py, pz), 16 * vx + 4 * vy + vz))
    return places


def voxel_classes():
    readers = {}
    for offset in range(TAPS):
        for pos, voxel in slab(offset):
            readers.setdefault(voxel, []).append((offset, pos))
    classes = {}
    for voxel in range(VOXELS):
        key = tuple(o for o, _ in readers[voxel])
        classes.setdefault(key, []).append((voxel, [pos for _, pos in readers[voxel]]))
    return classes


def kernel_body(sizes, scale, feat_h, occ_h, pairs_h, sends_h, weight_h, ker_h, cot_h,
                home_f, home_g, home_k, out_f, out_g, out_k,
                feat, occ, pairs_s, pairs_v, sends, weight, ker, cot, load_sem, gcols,
                mask, fnat, table, gnat, gvox, patch, pgrad, cols, tgrad, conv, wgrad,
                halo_out, halo_in, back_out, back_in, wsend, wrecv,
                core_in, half_in, tail_in, tail_sum, send_sem, recv_sem):
    nspace, ndp, cap, bricks, chan = sizes
    ls, ld = nspace.bit_length() - 1, ndp.bit_length() - 1
    own = bricks * VOXELS
    index = {"space": lax.axis_index("space"), "dp": lax.axis_index("dp")}

    def bit_of(bit):
        axis, level = bit
        return lax.rem(index[axis] // (1 << level), 2)

    def peer_index(bit):
        return index[bit[0]] + (1 - 2 * bit_of(bit)) * (1 << bit[1])

    loads = {}
    for n, (name, src, dst) in enumerate([
            ("occ", occ_h, occ), ("feat", feat_h, feat), ("sends", sends_h, sends),
            ("weight", weight_h, weight), ("cot", cot_h, cot), ("pairs_s", pairs_h, pairs_s),
            ("pairs_v", pairs_h, pairs_v), ("ker", ker_h, ker)]):
        loads[name] = pltpu.make_async_copy(src, dst, load_sem.at[n])
        loads[name].start()

    all_bits = [("dp", i) for i in range(ld)] + [("space", i) for i in range(ls)]
    barrier = pltpu.get_barrier_semaphore()
    for bit in all_bits:
        pl.semaphore_signal(barrier, inc=1, device_id={bit[0]: peer_index(bit)},
                            device_id_type=MESH)

    started = []

    def send(src, dst, bit):
        n = len(started)
        copy = pltpu.make_async_remote_copy(
            src_ref=src, dst_ref=dst, send_sem=send_sem.at[n], recv_sem=recv_sem.at[n],
            device_id={bit[0]: peer_index(bit)}, device_id_type=MESH)
        copy.start()
        started.append(copy)
        return copy

    loads["occ"].wait()
    for i in range(own // 128):
        row = occ[0:1, i * 128:(i + 1) * 128].astype(jnp.float32)
        mask[i * 128:(i + 1) * 128, :] = jnp.transpose(jnp.broadcast_to(row, (128, 128)))
    loads["feat"].wait()
    fnat[...] = feat[0].astype(jnp.float32) * mask[...]
    table[0:bricks] = fnat[...].reshape(bricks, VOXELS, chan)
    table[bricks + nspace * cap] = jnp.zeros((VOXELS, chan), jnp.float32)

    loads["sends"].wait()
    loads["weight"].wait()
    picks = []
    for level in range(ls):
        partner = peer_index(("space", level))
        for k in range(cap):
            chosen = sends[0, 0, partner * cap + k]
            picks.append(chosen)
            live = jnp.full((VOXELS, chan), chosen, jnp.int32) >= 0
            at = (level * cap + k) * VOXELS
            brick = table[jnp.maximum(chosen, 0)]
            halo_out[at:at + VOXELS, :] = jnp.where(live, brick, 0.0).astype(jnp.bfloat16)
    own_weight = weight[0].astype(jnp.float32)
    wsend[0] = jnp.full((8, 128), own_weight, jnp.float32)

    pl.semaphore_wait(barrier, len(all_bits))
    rows = cap * VOXELS
    halo = [send(halo_out.at[pl.ds(level * rows, rows)], halo_in.at[pl.ds(level * rows, rows)],
                 ("space", level)) for level in range(ls)]
    wcopy = send(wsend.at[0], wrecv.at[0], ("dp", 0))

    loads["cot"].wait()
    gnat[...] = cot[0].astype(jnp.float32) * mask[...]
    for v in range(VOXELS):
        gvox[v * 8:(v + 1) * 8, :] = gnat[pl.ds(v, bricks, stride=VOXELS), :]
    grad = gvox[...].astype(jnp.bfloat16)
    for pos, v in slab(13):
        patch[pos[0], pos[1], pos[2]] = fnat[pl.ds(v, bricks, stride=VOXELS), :]
    pgrad[...] = jnp.zeros(pgrad.shape, jnp.float32)

    plane = own // 4
    for px in range(6):
        for a in range(3):
            x = px - a
            gcols[px * plane:(px + 1) * plane, a * chan:(a + 1) * chan] = (
                grad[x * plane:(x + 1) * plane, :] if 0 <= x < 4
                else jnp.zeros((plane, chan), jnp.bfloat16))

    def spread(groups):
        for group in groups:
            b, c = group // 3, group % 3
            taps = [9 * a + group for a in range(3)]
            part = lax.dot_general(
                gcols[...],
                jnp.concatenate([ker[tap * chan:(tap + 1) * chan, :] for tap in taps], axis=1),
                (((1,), (1,)), ((), ())), preferred_element_type=jnp.float32)
            pgrad[:, b:b + 4, c:c + 4] += part.reshape(6, 4, 4, bricks, chan)

    loads["ker"].wait()
    spread(range(0, 3))

    for level in range(ls):
        halo[level].wait_recv()
        entry = bricks + peer_index(("space", level)) * cap
        for k in range(cap):
            at = level * rows + k * VOXELS
            table[entry + k] = halo_in[at:at + VOXELS, :].astype(jnp.float32)
    for level in range(ld):
        wcopy.wait_recv()
        wsend[level + 1] = wsend[level] + wrecv[level]
        if level + 1 < ld:
            wcopy = send(wsend.at[level + 1], wrecv.at[level + 1], ("dp", level + 1))
    loads["pairs_s"].wait()
    for b in range(bricks):
        for offset in range(TAPS):
            if offset != 13:
                entry = pairs_s[0, b, offset]
                for pos, v in slab(offset):
                    patch[pos[0], pos[1], pos[2], b:b + 1, :] = table[entry, v:v + 1, :]

    total_rows = TAPS * chan
    half_rows = total_rows // 2
    part_rows = half_rows // 3
    first, rest = all_bits[0], all_bits[1:]
    turn, tail = rest[:3], rest[3:]
    orders = [[turn[(p + j) % 3] for j in range(3)] for p in range(3)]
    mine = bit_of(first)

    def weigh(taps):
        for tap in taps:
            a, b, c = tap // 9, tap // 3 % 3, tap % 3
            cols[:, tap * chan:(tap + 1) * chan] = patch[a:a + 4, b:b + 4, c:c + 4].reshape(
                own, chan).astype(jnp.bfloat16)
        lo, hi = taps[0] * chan, (taps[-1] + 1) * chan
        wgrad[lo:hi, :] = own_weight * lax.dot_general(
            cols[:, lo:hi], grad, (((0,), (0,)), ((), ())), preferred_element_type=jnp.float32)

    def tile8(x):
        return pl.multiple_of(x, 8)

    units = part_rows // 64
    sizes_of = [(units + 1) // 2 * 64, units // 2 * 64]
    starts_of = [0, sizes_of[0]]
    offs = {(p, s): mine * half_rows + p * part_rows + starts_of[s]
            for s in range(2) for p in range(3)}
    flight = {}
    def reduce_stage(j, s, parts=range(3)):
        for p in parts:
            flight[p, s].wait_recv()
            size = sizes_of[s] >> min(j, 3)
            off = tile8(offs[p, s])
            tail_at = starts_of[s] >> 3
            if j == 0:
                wgrad[pl.ds(off, size), :] += core_in[p, starts_of[s]:starts_of[s] + size, :]
            elif j <= 3:
                at = starts_of[s] + sizes_of[s] - (sizes_of[s] >> (j - 1))
                wgrad[pl.ds(off, size), :] += half_in[p, at:at + size, :]
            else:
                i = j - 4
                held = (wgrad[pl.ds(off, size), :] if i == 0
                        else tail_sum[p, i - 1, tail_at:tail_at + size, :])
                tail_sum[p, i, tail_at:tail_at + size, :] = (
                    held + tail_in[p, i, tail_at:tail_at + size, :])
            if j < 3:
                bit = orders[p][j]
                half = size // 2
                at = starts_of[s] + sizes_of[s] - (sizes_of[s] >> j)
                other = tile8(offs[p, s] + (1 - bit_of(bit)) * half)
                flight[p, s] = send(wgrad.at[pl.ds(other, half)],
                                    half_in.at[p, pl.ds(at, half)], bit)
                offs[p, s] = offs[p, s] + bit_of(bit) * half
            elif j - 3 < len(tail):
                i = j - 3
                src = (wgrad.at[pl.ds(off, size)] if i == 0
                       else tail_sum.at[p, i - 1, pl.ds(tail_at, size)])
                flight[p, s] = send(src, tail_in.at[p, i, pl.ds(tail_at, size)], tail[i])

    for p in range(3):
        if p > 1:
            reduce_stage(0, 0, [p - 2])
            reduce_stage(0, 1, [p - 2])
        low_at = min(-(-p * part_rows // chan), half_rows // chan)
        high_at = -(-(half_rows + p * part_rows) // chan) if p else half_rows // chan
        low_end = min(-(-(p + 1) * part_rows // chan), half_rows // chan)
        high_end = -(-(half_rows + (p + 1) * part_rows) // chan)
        weigh(list(range(low_at, low_end)))
        weigh(list(range(high_at, high_end)))
        for s in range(2):
            src = tile8((1 - mine) * half_rows + p * part_rows + starts_of[s])
            flight[p, s] = send(wgrad.at[pl.ds(src, sizes_of[s])],
                                core_in.at[p, pl.ds(starts_of[s], sizes_of[s])], first)

    reduce_stage(0, 0, [1])
    reduce_stage(0, 1, [1])
    spread(range(3, 5))
    reduce_stage(0, 0, [2])
    reduce_stage(0, 1, [2])
    spread(range(5, 6))
    reduce_stage(1, 0)
    spread(range(6, 8))
    reduce_stage(1, 1)
    spread(range(8, 9))

    entries = tgrad.shape[0] // VOXELS
    lane = lax.broadcasted_iota(jnp.int32, (1, 128), 1)
    code = jnp.where(lane < bricks, lane, -1)
    for level in range(ls):
        for k in range(cap):
            name = bricks + peer_index(("space", level)) * cap + k
            code = jnp.where(lane == bricks + level * cap + k, name, code)
    loads["pairs_v"].wait()
    hits = {}
    for offset in range(TAPS):
        hit = pairs_v[0, :, offset:offset + 1] == code
        hits[offset] = jnp.where(hit, 1.0, 0.0).astype(jnp.float32)
    for turn_of, (offsets, voxels) in enumerate(voxel_classes().items()):
        if turn_of == 14:
            reduce_stage(2, 0)
        left = jnp.concatenate([hits[o] for o in offsets] * 2, axis=0).astype(jnp.bfloat16)
        right = jnp.concatenate(
            [jnp.concatenate([pgrad[pos[j][0], pos[j][1], pos[j][2]] for _, pos in voxels], axis=1)
             for j in range(len(offsets))], axis=0)
        high = right.astype(jnp.bfloat16)
        low = (right - high.astype(jnp.float32)).astype(jnp.bfloat16)
        sums = lax.dot_general(left, jnp.concatenate([high, low], axis=0),
                               (((0,), (0,)), ((), ())), preferred_element_type=jnp.float32)
        for n, (v, _) in enumerate(voxels):
            for t in range(0, entries, 8):
                tgrad[pl.ds(t * VOXELS + v, 8, stride=VOXELS), :] = sums[t:t + 8,
                                                                        n * chan:(n + 1) * chan]
    back_out[...] = tgrad[own:own + ls * rows, :].astype(jnp.bfloat16)
    back = [send(back_out.at[pl.ds(level * rows, rows)], back_in.at[pl.ds(level * rows, rows)],
                 ("space", level)) for level in range(ls)]

    reduce_stage(2, 1)
    third = TAPS // 3 * chan

    def convolve(i):
        return jnp.dot(cols[:, i * third:(i + 1) * third], ker[i * third:(i + 1) * third, :],
                       preferred_element_type=jnp.float32)

    total = wsend[ld][0:1, :]
    kernel_scale = (ndp / total) * scale

    to_core = {(p, s): [] for p in range(3) for s in range(2)}

    def to_other_core(p, s, off, size):
        at = pl.ds(tile8(off), size)
        to_core[p, s].append(send(out_k.at[at], out_k.at[at], first))

    def gather_start(j, s):
        for p in range(3):
            size = sizes_of[s] >> j
            off = tile8(offs[p, s])
            bit = orders[p][j - 1]
            flight[p, s] = send(out_k.at[pl.ds(off, size)], out_k.at[pl.ds(off, size)], bit)

    def gather_take(j, s):
        came = {}
        for p in range(3):
            flight[p, s].wait_recv()
            size = sizes_of[s] >> j
            bit = orders[p][j - 1]
            came[p] = (offs[p, s] + (1 - 2 * bit_of(bit)) * size, size)
            offs[p, s] = offs[p, s] - bit_of(bit) * size
        if j > 1:
            gather_start(j - 1, s)
        for p in range(3):
            to_other_core(p, s, *came[p])

    def finish(s):
        for j in range(len(tail)):
            reduce_stage(4 + j, s)
        last = sizes_of[s] >> 3
        tail_at = starts_of[s] >> 3
        for p in range(3):
            off = tile8(offs[p, s])
            held = (tail_sum[p, len(tail) - 1, tail_at:tail_at + last, :] if tail
                    else wgrad[pl.ds(off, last), :])
            out_k[pl.ds(off, last), :] = held * kernel_scale
        gather_start(3, s)
        for p in range(3):
            to_other_core(p, s, offs[p, s], last)

    conv[...] = convolve(0) + patch[1:5, 1:5, 1:5].reshape(own, chan)
    reduce_stage(3, 0)
    conv[...] += convolve(1)
    reduce_stage(3, 1)
    conv[...] += convolve(2)
    for v in range(VOXELS):
        gvox[pl.ds(v, bricks, stride=VOXELS), :] = conv[v * 8:(v + 1) * 8, :]
    out_f[0] = (gvox[...] * mask[...]).astype(jnp.bfloat16)
    homes = [pltpu.make_async_copy(out_f, home_f, load_sem.at[8])]
    homes[0].start()
    finish(0)
    for copy in back:
        copy.wait_recv()
    factor = own_weight * ndp / total

    def feature_grads(some):
        for b in some:
            lo, hi = b * VOXELS, (b + 1) * VOXELS
            held = gnat[lo:hi, :] + tgrad[lo:hi, :]
            for e, chosen in enumerate(picks):
                came = back_in[e * VOXELS:(e + 1) * VOXELS, :].astype(jnp.float32)
                here = jnp.full((VOXELS, chan), chosen, jnp.int32) == b
                held = held + jnp.where(here, came, 0.0)
            out_g[0, lo:hi, :] = (factor * (mask[lo:hi, :] * held)).astype(jnp.bfloat16)

    feature_grads(range(bricks // 2))
    finish(1)
    feature_grads(range(bricks // 2, bricks))
    homes.append(pltpu.make_async_copy(out_g, home_g, load_sem.at[9]))
    homes[1].start()
    for j in (3, 2, 1):
        for s in range(2):
            gather_take(j, s)

    def go_home(off, size):
        at = pl.ds(tile8(off), size)
        homes.append(pltpu.make_async_copy(out_k.at[at], home_k.at[at], load_sem.at[8 + len(homes)]))
        homes[-1].start()

    go_home(mine * half_rows, half_rows)
    for s in range(2):
        for p in range(3):
            for copy in to_core[p, s]:
                copy.wait_recv()
            go_home((1 - mine) * half_rows + p * part_rows + starts_of[s], sizes_of[s])
    for copy in homes:
        copy.wait()
    for copy in started:
        copy.wait_send()


def write_out(in_f, in_g, in_k, out_f, out_g, out_k, held_f, held_g, held_k, sems):
    rows = in_k.shape[0] // 4
    moves = [(in_f, held_f, out_f), (in_g, held_g, out_g)]
    for n in range(4):
        at = pl.ds(n * rows, rows)
        moves.append((in_k.at[at], held_k.at[at], out_k.at[at]))
    loads = [pltpu.make_async_copy(src, held, sems.at[2 * n])
             for n, (src, held, _) in enumerate(moves)]
    for copy in loads:
        copy.start()
    stores = [pltpu.make_async_copy(held, dst, sems.at[2 * n + 1])
              for n, (_, held, dst) in enumerate(moves)]
    for load, store in zip(loads, stores):
        load.wait()
        store.start()
    for copy in stores:
        copy.wait()


def on_device(features, occupancy, brick_pairs, send_lists, scan_weight, kernel, cotangent):
    nspace, ndp = lax.axis_size("space"), lax.axis_size("dp")
    own, chan = features.shape[1:]
    bricks = own // VOXELS
    cap = send_lists.shape[2] // nspace
    ls, ld = nspace.bit_length() - 1, ndp.bit_length() - 1
    entries = -(-(bricks + ls * cap) // 8) * 8
    rows = TAPS * chan
    part = rows // 6
    tail = max(ls + ld - 4, 1)
    copies = 2 * ls + ld + 6 * (1 + 3 + (ls + ld - 4) + 3 + 4)
    f32, bf16 = jnp.float32, jnp.bfloat16
    i32 = jnp.int32
    hbm = pl.BlockSpec(memory_space=pltpu.HBM)
    scale = 1.0 / math.sqrt(64.0 * bricks * nspace)
    results = pl.pallas_call(
        functools.partial(kernel_body, (nspace, ndp, cap, bricks, chan), scale),
        out_shape=(
            jax.ShapeDtypeStruct(features.shape, bf16),
            jax.ShapeDtypeStruct(features.shape, bf16),
            jax.ShapeDtypeStruct((rows, chan), f32),
        ),
        in_specs=[hbm] * 7,
        out_specs=(hbm, hbm, hbm),
        scratch_shapes=[
            pltpu.VMEM(features.shape, bf16),
            pltpu.VMEM(features.shape, bf16),
            pltpu.VMEM((rows, chan), f32),
            pltpu.VMEM(features.shape, bf16),
            pltpu.VMEM(occupancy.shape, i32),
            pltpu.SMEM(brick_pairs.shape, i32),
            pltpu.VMEM(brick_pairs.shape, i32),
            pltpu.SMEM(send_lists.shape, i32),
            pltpu.SMEM(scan_weight.shape, i32),
            pltpu.VMEM(kernel.shape, bf16),
            pltpu.VMEM(cotangent.shape, bf16),
            pltpu.SemaphoreType.DMA((17,)),
            pltpu.VMEM((own // 4 * 6, 3 * chan), bf16),
            pltpu.VMEM((own, chan), f32),
            pltpu.VMEM((own, chan), f32),
            pltpu.VMEM((bricks + nspace * cap + 1, VOXELS, chan), f32),
            pltpu.VMEM((own, chan), f32),
            pltpu.VMEM((own, chan), f32),
            pltpu.VMEM((6, 6, 6, bricks, chan), f32),
            pltpu.VMEM((6, 6, 6, bricks, chan), f32),
            pltpu.VMEM((own, rows), bf16),
            pltpu.VMEM((entries * VOXELS, chan), f32),
            pltpu.VMEM((own, chan), f32),
            pltpu.VMEM((rows, chan), f32),
            pltpu.VMEM((ls * cap * VOXELS, chan), bf16),
            pltpu.VMEM((ls * cap * VOXELS, chan), bf16),
            pltpu.VMEM((ls * cap * VOXELS, chan), bf16),
            pltpu.VMEM((ls * cap * VOXELS, chan), bf16),
            pltpu.VMEM((ld + 1, 8, 128), f32),
            pltpu.VMEM((ld, 8, 128), f32),
            pltpu.VMEM((3, part, chan), f32),
            pltpu.VMEM((3, part, chan), f32),
            pltpu.VMEM((3, tail, part // 8, chan), f32),
            pltpu.VMEM((3, tail, part // 8, chan), f32),
            pltpu.SemaphoreType.DMA((copies,)),
            pltpu.SemaphoreType.DMA((copies,)),
        ],
        compiler_params=pltpu.CompilerParams(
            collective_id=0, has_side_effects=True, vmem_limit_bytes=VMEM_GRANT
        ),
        cost_estimate=pl.CostEstimate(flops=6 * own * rows * chan, bytes_accessed=6 * 2**20,
                                      transcendentals=0),
    )(features, occupancy, brick_pairs, send_lists, scan_weight, kernel, cotangent)
    return pl.pallas_call(
        write_out,
        out_shape=tuple(jax.ShapeDtypeStruct(r.shape, r.dtype) for r in results),
        in_specs=[hbm] * 3,
        out_specs=(hbm, hbm, hbm),
        scratch_shapes=[pltpu.VMEM(features.shape, bf16), pltpu.VMEM(features.shape, bf16),
                        pltpu.VMEM((rows, chan), f32), pltpu.SemaphoreType.DMA((12,))],
        compiler_params=pltpu.CompilerParams(vmem_limit_bytes=VMEM_GRANT),
        cost_estimate=pl.CostEstimate(flops=0, bytes_accessed=4 * 2**20, transcendentals=0),
    )(*results)


def solution(mesh):
    return jax.shard_map(
        on_device,
        mesh=mesh,
        in_specs=(
            P("dp", "space", None),
            P("dp", "space"),
            P("dp", "space", None),
            P("dp", "space", None),
            P("dp"),
            P(),
            P("dp", "space", None),
        ),
        out_specs=(P("dp", "space", None), P("dp", "space", None), P()),
        check_vma=False,
    )
```

```python
import functools
import math

import jax
import jax.numpy as jnp
import numpy as np
from jax import lax
from jax.experimental import pallas as pl
from jax.experimental.pallas import tpu as pltpu
from jax.sharding import PartitionSpec as P

MESH = pl.DeviceIdType.MESH
VOXELS = 64
TAPS = 27
VMEM_GRANT = 64 * 2**20 - 2**16


def axis_places(step):
    return {-1: [(0, 3)], 0: [(1, 0), (2, 1), (3, 2), (4, 3)], 1: [(5, 0)]}[step]


def slab(offset):
    steps = (offset // 9 - 1, offset // 3 % 3 - 1, offset % 3 - 1)
    places = []
    for px, vx in axis_places(steps[0]):
        for py, vy in axis_places(steps[1]):
            for pz, vz in axis_places(steps[2]):
                places.append(((px, py, pz), 16 * vx + 4 * vy + vz))
    return places


def voxel_classes():
    readers = {}
    for offset in range(TAPS):
        for pos, voxel in slab(offset):
            readers.setdefault(voxel, []).append((offset, pos))
    classes = {}
    for voxel in range(VOXELS):
        key = tuple(o for o, _ in readers[voxel])
        classes.setdefault(key, []).append((voxel, [pos for _, pos in readers[voxel]]))
    return classes


def each(first, last, body):
    lax.fori_loop(first, last, lambda i, carry: (body(i), carry)[1], 0)


def tap_shifts(tap):
    return lax.div(tap, 9), lax.rem(lax.div(tap, 3), 3), lax.rem(tap, 3)


def kernel_body(sizes, scale, feat_h, occ_h, pairs_h, sends_h, weight_h, ker_h, cot_h,
                home_f, home_g, home_k, out_f, out_g, out_k,
                feat, occ, pairs_s, pairs_v, sends, weight, ker, cot, load_sem, gcols,
                mask, fnat, table, gnat, gvox, patch, pgrad, cols, tgrad, conv, wgrad,
                halo_out, halo_in, back_out, back_in, wsend, wrecv,
                core_in, half_in, tail_in, tail_sum, send_sem, recv_sem):
    nspace, ndp, cap, bricks, chan = sizes
    ls, ld = nspace.bit_length() - 1, ndp.bit_length() - 1
    own = bricks * VOXELS
    index = {"space": lax.axis_index("space"), "dp": lax.axis_index("dp")}

    def bit_of(bit):
        axis, level = bit
        return lax.rem(index[axis] // (1 << level), 2)

    def peer_index(bit):
        return index[bit[0]] + (1 - 2 * bit_of(bit)) * (1 << bit[1])

    loads = {}
    for n, (name, src, dst) in enumerate([
            ("occ", occ_h, occ), ("feat", feat_h, feat), ("sends", sends_h, sends),
            ("weight", weight_h, weight), ("cot", cot_h, cot), ("pairs_s", pairs_h, pairs_s),
            ("pairs_v", pairs_h, pairs_v), ("ker", ker_h, ker)]):
        loads[name] = pltpu.make_async_copy(src, dst, load_sem.at[n])
        loads[name].start()

    all_bits = [("dp", i) for i in range(ld)] + [("space", i) for i in range(ls)]
    barrier = pltpu.get_barrier_semaphore()
    for bit in all_bits:
        pl.semaphore_signal(barrier, inc=1, device_id={bit[0]: peer_index(bit)},
                            device_id_type=MESH)

    started = []

    def send(src, dst, bit):
        n = len(started)
        copy = pltpu.make_async_remote_copy(
            src_ref=src, dst_ref=dst, send_sem=send_sem.at[n], recv_sem=recv_sem.at[n],
            device_id={bit[0]: peer_index(bit)}, device_id_type=MESH)
        copy.start()
        started.append(copy)
        return copy

    loads["occ"].wait()
    for i in range(own // 128):
        row = occ[0:1, i * 128:(i + 1) * 128].astype(jnp.float32)
        mask[i * 128:(i + 1) * 128, :] = jnp.transpose(jnp.broadcast_to(row, (128, 128)))
    loads["feat"].wait()
    fnat[...] = feat[0].astype(jnp.float32) * mask[...]
    table[0:bricks] = fnat[...].reshape(bricks, VOXELS, chan)
    table[bricks + nspace * cap] = jnp.zeros((VOXELS, chan), jnp.float32)

    loads["sends"].wait()
    loads["weight"].wait()
    picks = []
    for level in range(ls):
        partner = peer_index(("space", level))
        for k in range(cap):
            chosen = sends[0, 0, partner * cap + k]
            picks.append(chosen)
            live = jnp.full((VOXELS, chan), chosen, jnp.int32) >= 0
            at = (level * cap + k) * VOXELS
            brick = table[jnp.maximum(chosen, 0)]
            halo_out[at:at + VOXELS, :] = jnp.where(live, brick, 0.0).astype(jnp.bfloat16)
    own_weight = weight[0].astype(jnp.float32)
    wsend[0] = jnp.full((8, 128), own_weight, jnp.float32)

    pl.semaphore_wait(barrier, len(all_bits))
    rows = cap * VOXELS
    halo = [send(halo_out.at[pl.ds(level * rows, rows)], halo_in.at[pl.ds(level * rows, rows)],
                 ("space", level)) for level in range(ls)]
    wcopy = send(wsend.at[0], wrecv.at[0], ("dp", 0))

    loads["cot"].wait()
    gnat[...] = cot[0].astype(jnp.float32) * mask[...]
    for v in range(VOXELS):
        gvox[v * 8:(v + 1) * 8, :] = gnat[pl.ds(v, bricks, stride=VOXELS), :]
    grad = gvox[...].astype(jnp.bfloat16)
    for pos, v in slab(13):
        patch[pos[0], pos[1], pos[2]] = fnat[pl.ds(v, bricks, stride=VOXELS), :]
    pgrad[...] = jnp.zeros(pgrad.shape, jnp.float32)

    plane = own // 4
    for px in range(6):
        for a in range(3):
            x = px - a
            gcols[px * plane:(px + 1) * plane, a * chan:(a + 1) * chan] = (
                grad[x * plane:(x + 1) * plane, :] if 0 <= x < 4
                else jnp.zeros((plane, chan), jnp.bfloat16))

    def spread(first, last):
        def one(group):
            b, c = lax.div(group, 3), lax.rem(group, 3)
            rows_of = [pl.ds(pl.multiple_of((9 * a + group) * chan, chan), chan) for a in range(3)]
            part = lax.dot_general(
                gcols[...], jnp.concatenate([ker[at, :] for at in rows_of], axis=1),
                (((1,), (1,)), ((), ())), preferred_element_type=jnp.float32)
            pgrad[:, pl.ds(b, 4), pl.ds(c, 4)] += part.reshape(6, 4, 4, bricks, chan)

        each(first, last, one)

    loads["ker"].wait()
    spread(0, 3)

    for level in range(ls):
        halo[level].wait_recv()
        entry = bricks + peer_index(("space", level)) * cap
        for k in range(cap):
            at = level * rows + k * VOXELS
            table[entry + k] = halo_in[at:at + VOXELS, :].astype(jnp.float32)
    for level in range(ld):
        wcopy.wait_recv()
        wsend[level + 1] = wsend[level] + wrecv[level]
        if level + 1 < ld:
            wcopy = send(wsend.at[level + 1], wrecv.at[level + 1], ("dp", level + 1))
    loads["pairs_s"].wait()

    def fill(b):
        for offset in range(TAPS):
            if offset != 13:
                entry = pairs_s[0, b, offset]
                for pos, v in slab(offset):
                    patch[pos[0], pos[1], pos[2], pl.ds(b, 1), :] = table[entry, v:v + 1, :]

    each(0, bricks, fill)

    total_rows = TAPS * chan
    half_rows = total_rows // 2
    part_rows = half_rows // 3
    first, rest = all_bits[0], all_bits[1:]
    turn, tail = rest[:3], rest[3:]
    orders = [[turn[(p + j) % 3] for j in range(3)] for p in range(3)]
    mine = bit_of(first)

    def weigh(first_tap, last_tap):
        def one(tap):
            a, b, c = tap_shifts(tap)
            at = pl.ds(pl.multiple_of(tap * chan, chan), chan)
            column = patch[pl.ds(a, 4), pl.ds(b, 4), pl.ds(c, 4)].reshape(own, chan).astype(
                jnp.bfloat16)
            cols[:, at] = column
            wgrad[at, :] = own_weight * lax.dot_general(
                column, gcols[0:own, 0:chan], (((0,), (0,)), ((), ())),
                preferred_element_type=jnp.float32)

        each(first_tap, last_tap, one)

    def tile8(x):
        return pl.multiple_of(x, 8)

    units = part_rows // 64
    sizes_of = [(units + 1) // 2 * 64, units // 2 * 64]
    starts_of = [0, sizes_of[0]]
    offs = {(p, s): mine * half_rows + p * part_rows + starts_of[s]
            for s in range(2) for p in range(3)}
    flight = {}
    def reduce_stage(j, s, parts=range(3)):
        for p in parts:
            flight[p, s].wait_recv()
            size = sizes_of[s] >> min(j, 3)
            off = tile8(offs[p, s])
            tail_at = starts_of[s] >> 3
            if j == 0:
                wgrad[pl.ds(off, size), :] += core_in[p, starts_of[s]:starts_of[s] + size, :]
            elif j <= 3:
                at = starts_of[s] + sizes_of[s] - (sizes_of[s] >> (j - 1))
                wgrad[pl.ds(off, size), :] += half_in[p, at:at + size, :]
            else:
                i = j - 4
                held = (wgrad[pl.ds(off, size), :] if i == 0
                        else tail_sum[p, i - 1, tail_at:tail_at + size, :])
                tail_sum[p, i, tail_at:tail_at + size, :] = (
                    held + tail_in[p, i, tail_at:tail_at + size, :])
            if j < 3:
                bit = orders[p][j]
                half = size // 2
                at = starts_of[s] + sizes_of[s] - (sizes_of[s] >> j)
                other = tile8(offs[p, s] + (1 - bit_of(bit)) * half)
                flight[p, s] = send(wgrad.at[pl.ds(other, half)],
                                    half_in.at[p, pl.ds(at, half)], bit)
                offs[p, s] = offs[p, s] + bit_of(bit) * half
            elif j - 3 < len(tail):
                i = j - 3
                src = (wgrad.at[pl.ds(off, size)] if i == 0
                       else tail_sum.at[p, i - 1, pl.ds(tail_at, size)])
                flight[p, s] = send(src, tail_in.at[p, i, pl.ds(tail_at, size)], tail[i])

    for p in range(3):
        if p > 1:
            reduce_stage(0, 0, [p - 2])
            reduce_stage(0, 1, [p - 2])
        low_at = min(-(-p * part_rows // chan), half_rows // chan)
        high_at = -(-(half_rows + p * part_rows) // chan) if p else half_rows // chan
        low_end = min(-(-(p + 1) * part_rows // chan), half_rows // chan)
        high_end = -(-(half_rows + (p + 1) * part_rows) // chan)
        weigh(low_at, low_end)
        weigh(high_at, high_end)
        for s in range(2):
            src = tile8((1 - mine) * half_rows + p * part_rows + starts_of[s])
            flight[p, s] = send(wgrad.at[pl.ds(src, sizes_of[s])],
                                core_in.at[p, pl.ds(starts_of[s], sizes_of[s])], first)

    reduce_stage(0, 0, [1])
    reduce_stage(0, 1, [1])
    spread(3, 5)
    reduce_stage(0, 0, [2])
    reduce_stage(0, 1, [2])
    spread(5, 6)
    reduce_stage(1, 0)
    spread(6, 8)
    reduce_stage(1, 1)
    spread(8, 9)

    entries = tgrad.shape[0] // VOXELS
    lane = lax.broadcasted_iota(jnp.int32, (1, 128), 1)
    code = jnp.where(lane < bricks, lane, -1)
    for level in range(ls):
        for k in range(cap):
            name = bricks + peer_index(("space", level)) * cap + k
            code = jnp.where(lane == bricks + level * cap + k, name, code)
    loads["pairs_v"].wait()
    hits = {}
    for offset in range(TAPS):
        hit = pairs_v[0, :, offset:offset + 1] == code
        hits[offset] = jnp.where(hit, 1.0, 0.0).astype(jnp.float32)
    for turn_of, (offsets, voxels) in enumerate(voxel_classes().items()):
        if turn_of == 14:
            reduce_stage(2, 0)
        left = jnp.concatenate([hits[o] for o in offsets] * 2, axis=0).astype(jnp.bfloat16)
        right = jnp.concatenate(
            [jnp.concatenate([pgrad[pos[j][0], pos[j][1], pos[j][2]] for _, pos in voxels], axis=1)
             for j in range(len(offsets))], axis=0)
        high = right.astype(jnp.bfloat16)
        low = (right - high.astype(jnp.float32)).astype(jnp.bfloat16)
        sums = lax.dot_general(left, jnp.concatenate([high, low], axis=0),
                               (((0,), (0,)), ((), ())), preferred_element_type=jnp.float32)
        for n, (v, _) in enumerate(voxels):
            for t in range(0, entries, 8):
                tgrad[pl.ds(t * VOXELS + v, 8, stride=VOXELS), :] = sums[t:t + 8,
                                                                        n * chan:(n + 1) * chan]
    back_out[...] = tgrad[own:own + ls * rows, :].astype(jnp.bfloat16)
    back = [send(back_out.at[pl.ds(level * rows, rows)], back_in.at[pl.ds(level * rows, rows)],
                 ("space", level)) for level in range(ls)]

    reduce_stage(2, 1)
    conv[...] = patch[1:5, 1:5, 1:5].reshape(own, chan)

    def convolve(first, last):
        def one(row):
            at = pl.ds(pl.multiple_of(row * 3 * chan, 3 * chan), 3 * chan)
            conv[...] += jnp.dot(cols[:, at], ker[at, :], preferred_element_type=jnp.float32)

        each(first, last, one)

    total = wsend[ld][0:1, :]
    kernel_scale = (ndp / total) * scale

    to_core = {(p, s): [] for p in range(3) for s in range(2)}

    def to_other_core(p, s, off, size):
        at = pl.ds(tile8(off), size)
        to_core[p, s].append(send(out_k.at[at], out_k.at[at], first))

    def gather_start(j, s):
        for p in range(3):
            size = sizes_of[s] >> j
            off = tile8(offs[p, s])
            bit = orders[p][j - 1]
            flight[p, s] = send(out_k.at[pl.ds(off, size)], out_k.at[pl.ds(off, size)], bit)

    def gather_take(j, s):
        came = {}
        for p in range(3):
            flight[p, s].wait_recv()
            size = sizes_of[s] >> j
            bit = orders[p][j - 1]
            came[p] = (offs[p, s] + (1 - 2 * bit_of(bit)) * size, size)
            offs[p, s] = offs[p, s] - bit_of(bit) * size
        if j > 1:
            gather_start(j - 1, s)
        for p in range(3):
            to_other_core(p, s, *came[p])

    def finish(s):
        for j in range(len(tail)):
            reduce_stage(4 + j, s)
        last = sizes_of[s] >> 3
        tail_at = starts_of[s] >> 3
        for p in range(3):
            off = tile8(offs[p, s])
            held = (tail_sum[p, len(tail) - 1, tail_at:tail_at + last, :] if tail
                    else wgrad[pl.ds(off, last), :])
            out_k[pl.ds(off, last), :] = held * kernel_scale
        gather_start(3, s)
        for p in range(3):
            to_other_core(p, s, offs[p, s], last)

    convolve(0, 3)
    reduce_stage(3, 0)
    convolve(3, 6)
    reduce_stage(3, 1)
    convolve(6, 9)
    for v in range(VOXELS):
        gvox[pl.ds(v, bricks, stride=VOXELS), :] = conv[v * 8:(v + 1) * 8, :]
    out_f[0] = (gvox[...] * mask[...]).astype(jnp.bfloat16)
    homes = [pltpu.make_async_copy(out_f, home_f, load_sem.at[8])]
    homes[0].start()
    finish(0)
    for copy in back:
        copy.wait_recv()
    factor = own_weight * ndp / total

    def feature_grads(first_brick, last_brick):
        def one(b):
            at = pl.ds(pl.multiple_of(b * VOXELS, VOXELS), VOXELS)
            held = gnat[at, :] + tgrad[at, :]
            for e, chosen in enumerate(picks):
                came = back_in[e * VOXELS:(e + 1) * VOXELS, :].astype(jnp.float32)
                here = jnp.full((VOXELS, chan), chosen, jnp.int32) == b
                held = held + jnp.where(here, came, 0.0)
            out_g[0, at, :] = (factor * (mask[at, :] * held)).astype(jnp.bfloat16)

        each(first_brick, last_brick, one)

    feature_grads(0, bricks // 2)
    finish(1)
    feature_grads(bricks // 2, bricks)
    homes.append(pltpu.make_async_copy(out_g, home_g, load_sem.at[9]))
    homes[1].start()
    for j in (3, 2, 1):
        for s in range(2):
            gather_take(j, s)

    def go_home(off, size):
        at = pl.ds(tile8(off), size)
        homes.append(pltpu.make_async_copy(out_k.at[at], home_k.at[at], load_sem.at[8 + len(homes)]))
        homes[-1].start()

    go_home(mine * half_rows, half_rows)
    for s in range(2):
        for p in range(3):
            for copy in to_core[p, s]:
                copy.wait_recv()
            go_home((1 - mine) * half_rows + p * part_rows + starts_of[s], sizes_of[s])
    for copy in homes:
        copy.wait()
    for copy in started:
        copy.wait_send()


def write_out(in_f, in_g, in_k, out_f, out_g, out_k, held_f, held_g, held_k, sems):
    rows = in_k.shape[0] // 4
    moves = [(in_f, held_f, out_f), (in_g, held_g, out_g)]
    for n in range(4):
        at = pl.ds(n * rows, rows)
        moves.append((in_k.at[at], held_k.at[at], out_k.at[at]))
    loads = [pltpu.make_async_copy(src, held, sems.at[2 * n])
             for n, (src, held, _) in enumerate(moves)]
    for copy in loads:
        copy.start()
    stores = [pltpu.make_async_copy(held, dst, sems.at[2 * n + 1])
              for n, (_, held, dst) in enumerate(moves)]
    for load, store in zip(loads, stores):
        load.wait()
        store.start()
    for copy in stores:
        copy.wait()


def on_device(features, occupancy, brick_pairs, send_lists, scan_weight, kernel, cotangent):
    nspace, ndp = lax.axis_size("space"), lax.axis_size("dp")
    own, chan = features.shape[1:]
    bricks = own // VOXELS
    cap = send_lists.shape[2] // nspace
    ls, ld = nspace.bit_length() - 1, ndp.bit_length() - 1
    entries = -(-(bricks + ls * cap) // 8) * 8
    rows = TAPS * chan
    part = rows // 6
    tail = max(ls + ld - 4, 1)
    copies = 2 * ls + ld + 6 * (1 + 3 + (ls + ld - 4) + 3 + 4)
    f32, bf16 = jnp.float32, jnp.bfloat16
    i32 = jnp.int32
    hbm = pl.BlockSpec(memory_space=pltpu.HBM)
    scale = 1.0 / math.sqrt(64.0 * bricks * nspace)
    results = pl.pallas_call(
        functools.partial(kernel_body, (nspace, ndp, cap, bricks, chan), scale),
        out_shape=(
            jax.ShapeDtypeStruct(features.shape, bf16),
            jax.ShapeDtypeStruct(features.shape, bf16),
            jax.ShapeDtypeStruct((rows, chan), f32),
        ),
        in_specs=[hbm] * 7,
        out_specs=(hbm, hbm, hbm),
        scratch_shapes=[
            pltpu.VMEM(features.shape, bf16),
            pltpu.VMEM(features.shape, bf16),
            pltpu.VMEM((rows, chan), f32),
            pltpu.VMEM(features.shape, bf16),
            pltpu.VMEM(occupancy.shape, i32),
            pltpu.SMEM(brick_pairs.shape, i32),
            pltpu.VMEM(brick_pairs.shape, i32),
            pltpu.SMEM(send_lists.shape, i32),
            pltpu.SMEM(scan_weight.shape, i32),
            pltpu.VMEM(kernel.shape, bf16),
            pltpu.VMEM(cotangent.shape, bf16),
            pltpu.SemaphoreType.DMA((17,)),
            pltpu.VMEM((own // 4 * 6, 3 * chan), bf16),
            pltpu.VMEM((own, chan), f32),
            pltpu.VMEM((own, chan), f32),
            pltpu.VMEM((bricks + nspace * cap + 1, VOXELS, chan), f32),
            pltpu.VMEM((own, chan), f32),
            pltpu.VMEM((own, chan), f32),
            pltpu.VMEM((6, 6, 6, bricks, chan), f32),
            pltpu.VMEM((6, 6, 6, bricks, chan), f32),
            pltpu.VMEM((own, rows), bf16),
            pltpu.VMEM((entries * VOXELS, chan), f32),
            pltpu.VMEM((own, chan), f32),
            pltpu.VMEM((rows, chan), f32),
            pltpu.VMEM((ls * cap * VOXELS, chan), bf16),
            pltpu.VMEM((ls * cap * VOXELS, chan), bf16),
            pltpu.VMEM((ls * cap * VOXELS, chan), bf16),
            pltpu.VMEM((ls * cap * VOXELS, chan), bf16),
            pltpu.VMEM((ld + 1, 8, 128), f32),
            pltpu.VMEM((ld, 8, 128), f32),
            pltpu.VMEM((3, part, chan), f32),
            pltpu.VMEM((3, part, chan), f32),
            pltpu.VMEM((3, tail, part // 8, chan), f32),
            pltpu.VMEM((3, tail, part // 8, chan), f32),
            pltpu.SemaphoreType.DMA((copies,)),
            pltpu.SemaphoreType.DMA((copies,)),
        ],
        compiler_params=pltpu.CompilerParams(
            collective_id=0, has_side_effects=True, vmem_limit_bytes=VMEM_GRANT
        ),
        cost_estimate=pl.CostEstimate(flops=6 * own * rows * chan, bytes_accessed=6 * 2**20,
                                      transcendentals=0),
    )(features, occupancy, brick_pairs, send_lists, scan_weight, kernel, cotangent)
    return pl.pallas_call(
        write_out,
        out_shape=tuple(jax.ShapeDtypeStruct(r.shape, r.dtype) for r in results),
        in_specs=[hbm] * 3,
        out_specs=(hbm, hbm, hbm),
        scratch_shapes=[pltpu.VMEM(features.shape, bf16), pltpu.VMEM(features.shape, bf16),
                        pltpu.VMEM((rows, chan), f32), pltpu.SemaphoreType.DMA((12,))],
        compiler_params=pltpu.CompilerParams(vmem_limit_bytes=VMEM_GRANT),
        cost_estimate=pl.CostEstimate(flops=0, bytes_accessed=4 * 2**20, transcendentals=0),
    )(*results)


def solution(mesh):
    return jax.shard_map(
        on_device,
        mesh=mesh,
        in_specs=(
            P("dp", "space", None),
            P("dp", "space"),
            P("dp", "space", None),
            P("dp", "space", None),
            P("dp"),
            P(),
            P("dp", "space", None),
        ),
        out_specs=(P("dp", "space", None), P("dp", "space", None), P()),
        check_vma=False,
    )
```

```python
import functools
import math

import jax
import jax.numpy as jnp
import numpy as np
from jax import lax
from jax.experimental import pallas as pl
from jax.experimental.pallas import tpu as pltpu
from jax.sharding import PartitionSpec as P

MESH = pl.DeviceIdType.MESH
VOXELS = 64
TAPS = 27
VMEM_GRANT = 64 * 2**20 - 2**16


def axis_places(step):
    return {-1: [(0, 3)], 0: [(1, 0), (2, 1), (3, 2), (4, 3)], 1: [(5, 0)]}[step]


def slab(offset):
    steps = (offset // 9 - 1, offset // 3 % 3 - 1, offset % 3 - 1)
    places = []
    for px, vx in axis_places(steps[0]):
        for py, vy in axis_places(steps[1]):
            for pz, vz in axis_places(steps[2]):
                places.append(((px, py, pz), 16 * vx + 4 * vy + vz))
    return places


def voxel_classes():
    readers = {}
    for offset in range(TAPS):
        for pos, voxel in slab(offset):
            readers.setdefault(voxel, []).append((offset, pos))
    classes = {}
    for voxel in range(VOXELS):
        key = tuple(o for o, _ in readers[voxel])
        classes.setdefault(key, []).append((voxel, [pos for _, pos in readers[voxel]]))
    return classes


def kernel_body(sizes, scale, feat_h, occ_h, pairs_h, sends_h, weight_h, ker_h, cot_h,
                home_f, home_g, home_k, out_f, out_g, out_k,
                feat, occ, pairs_s, pairs_v, sends, weight, ker, cot, load_sem, gcols,
                mask, fnat, table, gnat, gvox, patch, pgrad, cols, tgrad, conv, wgrad,
                halo_out, halo_in, back_out, back_in, wsend, wrecv,
                core_in, half_in, tail_in, tail_sum, send_sem, recv_sem):
    nspace, ndp, cap, bricks, chan = sizes
    ls, ld = nspace.bit_length() - 1, ndp.bit_length() - 1
    own = bricks * VOXELS
    index = {"space": lax.axis_index("space"), "dp": lax.axis_index("dp")}

    def bit_of(bit):
        axis, level = bit
        return lax.rem(index[axis] // (1 << level), 2)

    def peer_index(bit):
        return index[bit[0]] + (1 - 2 * bit_of(bit)) * (1 << bit[1])

    loads = {}
    for n, (name, src, dst) in enumerate([
            ("occ", occ_h, occ), ("feat", feat_h, feat), ("sends", sends_h, sends),
            ("weight", weight_h, weight), ("cot", cot_h, cot), ("pairs_s", pairs_h, pairs_s),
            ("pairs_v", pairs_h, pairs_v), ("ker", ker_h, ker)]):
        loads[name] = pltpu.make_async_copy(src, dst, load_sem.at[n])
        loads[name].start()

    all_bits = [("dp", i) for i in range(ld)] + [("space", i) for i in range(ls)]
    barrier = pltpu.get_barrier_semaphore()
    for bit in all_bits:
        pl.semaphore_signal(barrier, inc=1, device_id={bit[0]: peer_index(bit)},
                            device_id_type=MESH)

    started = []

    def send(src, dst, bit):
        n = len(started)
        copy = pltpu.make_async_remote_copy(
            src_ref=src, dst_ref=dst, send_sem=send_sem.at[n], recv_sem=recv_sem.at[n],
            device_id={bit[0]: peer_index(bit)}, device_id_type=MESH)
        copy.start()
        started.append(copy)
        return copy

    loads["occ"].wait()
    for i in range(own // 128):
        row = occ[0:1, i * 128:(i + 1) * 128].astype(jnp.float32)
        mask[i * 128:(i + 1) * 128, :] = jnp.transpose(jnp.broadcast_to(row, (128, 128)))
    loads["feat"].wait()
    fnat[...] = feat[0].astype(jnp.float32) * mask[...]
    table[0:bricks] = fnat[...].reshape(bricks, VOXELS, chan)
    table[bricks + nspace * cap] = jnp.zeros((VOXELS, chan), jnp.float32)

    loads["sends"].wait()
    loads["weight"].wait()
    picks = []
    for level in range(ls):
        partner = peer_index(("space", level))
        for k in range(cap):
            chosen = sends[0, 0, partner * cap + k]
            picks.append(chosen)
            live = jnp.full((VOXELS, chan), chosen, jnp.int32) >= 0
            at = (level * cap + k) * VOXELS
            brick = table[jnp.maximum(chosen, 0)]
            halo_out[at:at + VOXELS, :] = jnp.where(live, brick, 0.0).astype(jnp.bfloat16)
    own_weight = weight[0].astype(jnp.float32)
    wsend[0] = jnp.full((8, 128), own_weight, jnp.float32)

    pl.semaphore_wait(barrier, len(all_bits))
    rows = cap * VOXELS
    halo = [send(halo_out.at[pl.ds(level * rows, rows)], halo_in.at[pl.ds(level * rows, rows)],
                 ("space", level)) for level in range(ls)]
    wcopy = send(wsend.at[0], wrecv.at[0], ("dp", 0))

    loads["cot"].wait()
    gnat[...] = cot[0].astype(jnp.float32) * mask[...]
    for v in range(VOXELS):
        gvox[v * 8:(v + 1) * 8, :] = gnat[pl.ds(v, bricks, stride=VOXELS), :]
    grad = gvox[...].astype(jnp.bfloat16)
    for pos, v in slab(13):
        patch[pos[0], pos[1], pos[2]] = fnat[pl.ds(v, bricks, stride=VOXELS), :]
    pgrad[...] = jnp.zeros(pgrad.shape, jnp.float32)

    plane = own // 4
    for px in range(6):
        for a in range(3):
            x = px - a
            gcols[px * plane:(px + 1) * plane, a * chan:(a + 1) * chan] = (
                grad[x * plane:(x + 1) * plane, :] if 0 <= x < 4
                else jnp.zeros((plane, chan), jnp.bfloat16))

    def spread(groups):
        for group in groups:
            b, c = group // 3, group % 3
            taps = [9 * a + group for a in range(3)]
            part = lax.dot_general(
                gcols[...],
                jnp.concatenate([ker[tap * chan:(tap + 1) * chan, :] for tap in taps], axis=1),
                (((1,), (1,)), ((), ())), preferred_element_type=jnp.float32)
            pgrad[:, b:b + 4, c:c + 4] += part.reshape(6, 4, 4, bricks, chan)

    loads["ker"].wait()
    spread(range(0, 3))

    for level in range(ls):
        halo[level].wait_recv()
        entry = bricks + peer_index(("space", level)) * cap
        for k in range(cap):
            at = level * rows + k * VOXELS
            table[entry + k] = halo_in[at:at + VOXELS, :].astype(jnp.float32)
    for level in range(ld):
        wcopy.wait_recv()
        wsend[level + 1] = wsend[level] + wrecv[level]
        if level + 1 < ld:
            wcopy = send(wsend.at[level + 1], wrecv.at[level + 1], ("dp", level + 1))
    loads["pairs_s"].wait()
    for b in range(bricks):
        for offset in range(TAPS):
            if offset != 13:
                entry = pairs_s[0, b, offset]
                for pos, v in slab(offset):
                    patch[pos[0], pos[1], pos[2], b:b + 1, :] = table[entry, v:v + 1, :]

    total_rows = TAPS * chan
    half_rows = total_rows // 2
    part_rows = half_rows // 3
    first, rest = all_bits[0], all_bits[1:]
    turn, tail = rest[:3], rest[3:]
    orders = [[turn[(p + j) % 3] for j in range(3)] for p in range(3)]
    mine = bit_of(first)

    def weigh(taps):
        for tap in taps:
            a, b, c = tap // 9, tap // 3 % 3, tap % 3
            cols[:, tap * chan:(tap + 1) * chan] = patch[a:a + 4, b:b + 4, c:c + 4].reshape(
                own, chan).astype(jnp.bfloat16)
        lo, hi = taps[0] * chan, (taps[-1] + 1) * chan
        wgrad[lo:hi, :] = own_weight * lax.dot_general(
            cols[:, lo:hi], grad, (((0,), (0,)), ((), ())), preferred_element_type=jnp.float32)

    def tile8(x):
        return pl.multiple_of(x, 8)

    units = part_rows // 64
    sizes_of = [(units + 1) // 2 * 64, units // 2 * 64]
    starts_of = [0, sizes_of[0]]
    offs = {(p, s): mine * half_rows + p * part_rows + starts_of[s]
            for s in range(2) for p in range(3)}
    flight = {}
    def reduce_stage(j, s, parts=range(3)):
        for p in parts:
            flight[p, s].wait_recv()
            size = sizes_of[s] >> min(j, 3)
            off = tile8(offs[p, s])
            tail_at = starts_of[s] >> 3
            if j == 0:
                wgrad[pl.ds(off, size), :] += core_in[p, starts_of[s]:starts_of[s] + size, :]
            elif j <= 3:
                at = starts_of[s] + sizes_of[s] - (sizes_of[s] >> (j - 1))
                wgrad[pl.ds(off, size), :] += half_in[p, at:at + size, :]
            else:
                i = j - 4
                held = (wgrad[pl.ds(off, size), :] if i == 0
                        else tail_sum[p, i - 1, tail_at:tail_at + size, :])
                tail_sum[p, i, tail_at:tail_at + size, :] = (
                    held + tail_in[p, i, tail_at:tail_at + size, :])
            if j < 3:
                bit = orders[p][j]
                half = size // 2
                at = starts_of[s] + sizes_of[s] - (sizes_of[s] >> j)
                other = tile8(offs[p, s] + (1 - bit_of(bit)) * half)
                flight[p, s] = send(wgrad.at[pl.ds(other, half)],
                                    half_in.at[p, pl.ds(at, half)], bit)
                offs[p, s] = offs[p, s] + bit_of(bit) * half
            elif j - 3 < len(tail):
                i = j - 3
                src = (wgrad.at[pl.ds(off, size)] if i == 0
                       else tail_sum.at[p, i - 1, pl.ds(tail_at, size)])
                flight[p, s] = send(src, tail_in.at[p, i, pl.ds(tail_at, size)], tail[i])

    for p in range(3):
        if p > 1:
            reduce_stage(0, 0, [p - 2])
            reduce_stage(0, 1, [p - 2])
        low_at = min(-(-p * part_rows // chan), half_rows // chan)
        high_at = -(-(half_rows + p * part_rows) // chan) if p else half_rows // chan
        low_end = min(-(-(p + 1) * part_rows // chan), half_rows // chan)
        high_end = -(-(half_rows + (p + 1) * part_rows) // chan)
        weigh(list(range(low_at, low_end)))
        weigh(list(range(high_at, high_end)))
        for s in range(2):
            src = tile8((1 - mine) * half_rows + p * part_rows + starts_of[s])
            flight[p, s] = send(wgrad.at[pl.ds(src, sizes_of[s])],
                                core_in.at[p, pl.ds(starts_of[s], sizes_of[s])], first)

    reduce_stage(0, 0, [1])
    reduce_stage(0, 1, [1])
    spread(range(3, 5))
    reduce_stage(0, 0, [2])
    reduce_stage(0, 1, [2])
    spread(range(5, 6))
    reduce_stage(1, 0)
    spread(range(6, 8))
    reduce_stage(1, 1)
    spread(range(8, 9))

    entries = tgrad.shape[0] // VOXELS
    lane = lax.broadcasted_iota(jnp.int32, (1, 128), 1)
    code = jnp.where(lane < bricks, lane, -1)
    for level in range(ls):
        for k in range(cap):
            name = bricks + peer_index(("space", level)) * cap + k
            code = jnp.where(lane == bricks + level * cap + k, name, code)
    loads["pairs_v"].wait()
    hits = {}
    for offset in range(TAPS):
        hit = pairs_v[0, :, offset:offset + 1] == code
        hits[offset] = jnp.where(hit, 1.0, 0.0).astype(jnp.float32)
    for turn_of, (offsets, voxels) in enumerate(voxel_classes().items()):
        if turn_of == 14:
            reduce_stage(2, 0)
            reduce_stage(2, 1)
        left = jnp.concatenate([hits[o] for o in offsets] * 2, axis=0).astype(jnp.bfloat16)
        right = jnp.concatenate(
            [jnp.concatenate([pgrad[pos[j][0], pos[j][1], pos[j][2]] for _, pos in voxels], axis=1)
             for j in range(len(offsets))], axis=0)
        high = right.astype(jnp.bfloat16)
        low = (right - high.astype(jnp.float32)).astype(jnp.bfloat16)
        sums = lax.dot_general(left, jnp.concatenate([high, low], axis=0),
                               (((0,), (0,)), ((), ())), preferred_element_type=jnp.float32)
        for n, (v, _) in enumerate(voxels):
            for t in range(0, entries, 8):
                tgrad[pl.ds(t * VOXELS + v, 8, stride=VOXELS), :] = sums[t:t + 8,
                                                                        n * chan:(n + 1) * chan]
    back_out[...] = tgrad[own:own + ls * rows, :].astype(jnp.bfloat16)
    back = [send(back_out.at[pl.ds(level * rows, rows)], back_in.at[pl.ds(level * rows, rows)],
                 ("space", level)) for level in range(ls)]

    third = TAPS // 3 * chan

    def convolve(i):
        return jnp.dot(cols[:, i * third:(i + 1) * third], ker[i * third:(i + 1) * third, :],
                       preferred_element_type=jnp.float32)

    total = wsend[ld][0:1, :]
    kernel_scale = (ndp / total) * scale

    to_core = {(p, s): [] for p in range(3) for s in range(2)}

    def to_other_core(p, s, off, size):
        at = pl.ds(tile8(off), size)
        to_core[p, s].append(send(out_k.at[at], out_k.at[at], first))

    def gather_start(j, s):
        for p in range(3):
            size = sizes_of[s] >> j
            off = tile8(offs[p, s])
            bit = orders[p][j - 1]
            flight[p, s] = send(out_k.at[pl.ds(off, size)], out_k.at[pl.ds(off, size)], bit)

    def gather_take(j, s):
        came = {}
        for p in range(3):
            flight[p, s].wait_recv()
            size = sizes_of[s] >> j
            bit = orders[p][j - 1]
            came[p] = (offs[p, s] + (1 - 2 * bit_of(bit)) * size, size)
            offs[p, s] = offs[p, s] - bit_of(bit) * size
        if j > 1:
            gather_start(j - 1, s)
        for p in range(3):
            to_other_core(p, s, *came[p])

    def finish(s):
        for j in range(len(tail)):
            reduce_stage(4 + j, s)
        last = sizes_of[s] >> 3
        tail_at = starts_of[s] >> 3
        for p in range(3):
            off = tile8(offs[p, s])
            held = (tail_sum[p, len(tail) - 1, tail_at:tail_at + last, :] if tail
                    else wgrad[pl.ds(off, last), :])
            out_k[pl.ds(off, last), :] = held * kernel_scale
        gather_start(3, s)
        for p in range(3):
            to_other_core(p, s, offs[p, s], last)

    reduce_stage(3, 0)
    reduce_stage(3, 1)
    conv[...] = convolve(0) + patch[1:5, 1:5, 1:5].reshape(own, chan)
    finish(0)
    conv[...] += convolve(1)
    finish(1)
    gather_take(3, 0)
    gather_take(3, 1)
    conv[...] += convolve(2)
    gather_take(2, 0)
    gather_take(2, 1)
    for v in range(VOXELS):
        gvox[pl.ds(v, bricks, stride=VOXELS), :] = conv[v * 8:(v + 1) * 8, :]
    out_f[0] = (gvox[...] * mask[...]).astype(jnp.bfloat16)
    homes = [pltpu.make_async_copy(out_f, home_f, load_sem.at[8])]
    homes[0].start()
    for copy in back:
        copy.wait_recv()
    factor = own_weight * ndp / total

    def feature_grads(some):
        for b in some:
            lo, hi = b * VOXELS, (b + 1) * VOXELS
            held = gnat[lo:hi, :] + tgrad[lo:hi, :]
            for e, chosen in enumerate(picks):
                came = back_in[e * VOXELS:(e + 1) * VOXELS, :].astype(jnp.float32)
                here = jnp.full((VOXELS, chan), chosen, jnp.int32) == b
                held = held + jnp.where(here, came, 0.0)
            out_g[0, lo:hi, :] = (factor * (mask[lo:hi, :] * held)).astype(jnp.bfloat16)

    feature_grads(range(bricks))
    homes.append(pltpu.make_async_copy(out_g, home_g, load_sem.at[9]))
    homes[1].start()
    gather_take(1, 0)
    gather_take(1, 1)

    def go_home(off, size):
        at = pl.ds(tile8(off), size)
        homes.append(pltpu.make_async_copy(out_k.at[at], home_k.at[at], load_sem.at[8 + len(homes)]))
        homes[-1].start()

    go_home(mine * half_rows, half_rows)
    for s in range(2):
        for p in range(3):
            for copy in to_core[p, s]:
                copy.wait_recv()
            go_home((1 - mine) * half_rows + p * part_rows + starts_of[s], sizes_of[s])
    for copy in homes:
        copy.wait()
    for copy in started:
        copy.wait_send()


def write_out(in_f, in_g, in_k, out_f, out_g, out_k, held_f, held_g, held_k, sems):
    rows = in_k.shape[0] // 4
    moves = [(in_f, held_f, out_f), (in_g, held_g, out_g)]
    for n in range(4):
        at = pl.ds(n * rows, rows)
        moves.append((in_k.at[at], held_k.at[at], out_k.at[at]))
    loads = [pltpu.make_async_copy(src, held, sems.at[2 * n])
             for n, (src, held, _) in enumerate(moves)]
    for copy in loads:
        copy.start()
    stores = [pltpu.make_async_copy(held, dst, sems.at[2 * n + 1])
              for n, (_, held, dst) in enumerate(moves)]
    for load, store in zip(loads, stores):
        load.wait()
        store.start()
    for copy in stores:
        copy.wait()


def on_device(features, occupancy, brick_pairs, send_lists, scan_weight, kernel, cotangent):
    nspace, ndp = lax.axis_size("space"), lax.axis_size("dp")
    own, chan = features.shape[1:]
    bricks = own // VOXELS
    cap = send_lists.shape[2] // nspace
    ls, ld = nspace.bit_length() - 1, ndp.bit_length() - 1
    entries = -(-(bricks + ls * cap) // 8) * 8
    rows = TAPS * chan
    part = rows // 6
    tail = max(ls + ld - 4, 1)
    copies = 2 * ls + ld + 6 * (1 + 3 + (ls + ld - 4) + 3 + 4)
    f32, bf16 = jnp.float32, jnp.bfloat16
    i32 = jnp.int32
    hbm = pl.BlockSpec(memory_space=pltpu.HBM)
    scale = 1.0 / math.sqrt(64.0 * bricks * nspace)
    results = pl.pallas_call(
        functools.partial(kernel_body, (nspace, ndp, cap, bricks, chan), scale),
        out_shape=(
            jax.ShapeDtypeStruct(features.shape, bf16),
            jax.ShapeDtypeStruct(features.shape, bf16),
            jax.ShapeDtypeStruct((rows, chan), f32),
        ),
        in_specs=[hbm] * 7,
        out_specs=(hbm, hbm, hbm),
        scratch_shapes=[
            pltpu.VMEM(features.shape, bf16),
            pltpu.VMEM(features.shape, bf16),
            pltpu.VMEM((rows, chan), f32),
            pltpu.VMEM(features.shape, bf16),
            pltpu.VMEM(occupancy.shape, i32),
            pltpu.SMEM(brick_pairs.shape, i32),
            pltpu.VMEM(brick_pairs.shape, i32),
            pltpu.SMEM(send_lists.shape, i32),
            pltpu.SMEM(scan_weight.shape, i32),
            pltpu.VMEM(kernel.shape, bf16),
            pltpu.VMEM(cotangent.shape, bf16),
            pltpu.SemaphoreType.DMA((17,)),
            pltpu.VMEM((own // 4 * 6, 3 * chan), bf16),
            pltpu.VMEM((own, chan), f32),
            pltpu.VMEM((own, chan), f32),
            pltpu.VMEM((bricks + nspace * cap + 1, VOXELS, chan), f32),
            pltpu.VMEM((own, chan), f32),
            pltpu.VMEM((own, chan), f32),
            pltpu.VMEM((6, 6, 6, bricks, chan), f32),
            pltpu.VMEM((6, 6, 6, bricks, chan), f32),
            pltpu.VMEM((own, rows), bf16),
            pltpu.VMEM((entries * VOXELS, chan), f32),
            pltpu.VMEM((own, chan), f32),
            pltpu.VMEM((rows, chan), f32),
            pltpu.VMEM((ls * cap * VOXELS, chan), bf16),
            pltpu.VMEM((ls * cap * VOXELS, chan), bf16),
            pltpu.VMEM((ls * cap * VOXELS, chan), bf16),
            pltpu.VMEM((ls * cap * VOXELS, chan), bf16),
            pltpu.VMEM((ld + 1, 8, 128), f32),
            pltpu.VMEM((ld, 8, 128), f32),
            pltpu.VMEM((3, part, chan), f32),
            pltpu.VMEM((3, part, chan), f32),
            pltpu.VMEM((3, tail, part // 8, chan), f32),
            pltpu.VMEM((3, tail, part // 8, chan), f32),
            pltpu.SemaphoreType.DMA((copies,)),
            pltpu.SemaphoreType.DMA((copies,)),
        ],
        compiler_params=pltpu.CompilerParams(
            collective_id=0, has_side_effects=True, vmem_limit_bytes=VMEM_GRANT
        ),
        cost_estimate=pl.CostEstimate(flops=6 * own * rows * chan, bytes_accessed=6 * 2**20,
                                      transcendentals=0),
    )(features, occupancy, brick_pairs, send_lists, scan_weight, kernel, cotangent)
    return pl.pallas_call(
        write_out,
        out_shape=tuple(jax.ShapeDtypeStruct(r.shape, r.dtype) for r in results),
        in_specs=[hbm] * 3,
        out_specs=(hbm, hbm, hbm),
        scratch_shapes=[pltpu.VMEM(features.shape, bf16), pltpu.VMEM(features.shape, bf16),
                        pltpu.VMEM((rows, chan), f32), pltpu.SemaphoreType.DMA((12,))],
        compiler_params=pltpu.CompilerParams(vmem_limit_bytes=VMEM_GRANT),
        cost_estimate=pl.CostEstimate(flops=0, bytes_accessed=4 * 2**20, transcendentals=0),
    )(*results)


def solution(mesh):
    return jax.shard_map(
        on_device,
        mesh=mesh,
        in_specs=(
            P("dp", "space", None),
            P("dp", "space"),
            P("dp", "space", None),
            P("dp", "space", None),
            P("dp"),
            P(),
            P("dp", "space", None),
        ),
        out_specs=(P("dp", "space", None), P("dp", "space", None), P()),
        check_vma=False,
    )
```
